768 devices in a mesh: dp: 12 (over z), table: 64 (over y, x, core).
Axes of the slice: x: 4, y: 8, z: 12, core: 2. Of those that a mesh axis runs over, the one named last changes fastest.
Arguments:
- item_ids: int32 [196608], P(('dp', 'table')), may hold values from 0 to 65535, as said below
- lengths: int32 [768, 4], P(('dp', 'table')), may hold values from 1 to 128, 256 in all within a row
- item_table: bfloat16 [65536, 1024], P('table'), may hold values from -6 to 6
- admitted: int32 [65536], P('table'), may hold values 0 or 1
- input_weight: bfloat16 [1024, 2048], replicated, may hold values from -0.1875 to 0.1875
- output_weight: bfloat16 [512, 1024], replicated, may hold values from -0.25 to 0.25
- out_grad: bfloat16 [196608, 1024], P(('dp', 'table')), may hold values from -6 to 6
Outputs:
- layer_out: bfloat16 [196608, 1024], P(('dp', 'table'))
- embed_grad: float32 [196608, 1024], P(('dp', 'table'))
- weight_grad: float32 [512, 1024], P('table')
The draws below stay inside these ranges and needn't reach their ends.
Inputs may be any that keep to these rules, and one draw needn't show every extreme that they name: `item_ids`: in each aligned block of 256 ids, at most 8 lie in one table shard (ids k * 1024 to (k + 1) * 1024 - 1); in each group of 64 consecutive blocks one shard receives exactly 8 ids from every block of the group. The 4 lengths of a device sum to 256.
All inputs are finite; a program needn't handle non-finite values. No bound on the sum of `admitted` on one device may be relied on, other than what follows from the above.
Results may differ from the reference program's by a relative error of at most 0.0085.
Values may be sent and summed in bfloat16 or wider, within the bound.
A program may use at most 64 MiB of HBM per device.

```python
import math
import jax
import jax.numpy as jnp
import numpy as np
from jax import lax

D = 1024
HEADS = 4
WIDTH = 512
TOK_DEV = 256
SEQ_DEV = 4
MOST = 128
ROWS_DEV = 1024
CAP = 8
ROWS = 65536
TOKENS = 196608
N_DP = 12
N_TABLE = 64
DEVICES = 768


def draw_item_ids(key, part):
    key = jax.random.fold_in(key, 11)
    key_hot, key_spread, key_order, key_rows = jax.random.split(key, 4)
    groups = N_DP
    members = N_TABLE
    blocks = groups * members
    hot_shard = jnp.repeat(jax.random.randint(key_hot, (groups,), 0, members), members)
    spread_keys = jax.random.split(key_spread, blocks)
    spread = jax.vmap(lambda subkey: jax.random.permutation(subkey, (members - 1) * CAP)[:TOK_DEV - CAP])(spread_keys)
    others = (spread // CAP + hot_shard[:, None] + 1) % members
    shard_ids = jnp.concatenate([jnp.broadcast_to(hot_shard[:, None], (blocks, CAP)), others], axis=1)
    order_keys = jax.random.split(key_order, blocks)
    shuffle = jax.vmap(lambda subkey: jax.random.permutation(subkey, TOK_DEV))(order_keys)
    shard_ids = jnp.take_along_axis(shard_ids, shuffle, axis=1)
    row_local = jax.random.randint(key_rows, (blocks, TOK_DEV), 0, ROWS_DEV)
    return (shard_ids * ROWS_DEV + row_local).reshape(-1).astype(jnp.int32)


def place_ends(values, rng, low, top_value):
    index_at = [jax.random.randint(jax.random.fold_in(rng, axis), (), 0, length) for axis, length in enumerate(values.shape)]
    widest = values.shape.index(max(values.shape))
    beside = index_at[:widest] + [(index_at[widest] + 1) % values.shape[widest]] + index_at[widest + 1:]
    return values.at[tuple(index_at)].set(low).at[tuple(beside)].set(top_value)


def levels(key, shape, cuts, low, largest):
    def one(axis_at, shards_of):
        draws = jax.random.uniform(jax.random.fold_in(jax.random.fold_in(key, 6), axis_at), (shards_of,), jnp.float32, low / len(cuts), largest / len(cuts))
        return jnp.repeat(jnp.exp(draws), shape[axis_at] // shards_of).reshape((-1,) + (1,) * (len(shape) - axis_at - 1))

    loudness = one(*cuts[0])
    for cut in cuts[1:]:
        loudness = loudness * one(*cut)
    return loudness


def profile(amount, total, reach, slope):
    portions = [(1 << 20) // math.isqrt(grade ** slope) + 1 for grade in range(2, amount + 1)]
    rest, holding = total - reach - (amount - 1), [1] * (amount - 1)
    while rest > 0:
        free = [i for i in range(amount - 1) if holding[i] < reach]
        whole, left = sum([portions[i] for i in free]), rest
        for i in free:
            more = min(reach - holding[i], max(1, left * portions[i] // whole), rest)
            holding[i] = holding[i] + more
            rest = rest - more
    return np.array([reach] + holding)


def uneven(stream_key, count, total, limit, lean):
    if count == 2:
        one = jax.random.randint(stream_key, (), max(1, total - limit), min(limit, total - 1) + 1)
        return jnp.stack([one, total - one])
    sizes = jnp.asarray(profile(count, total, limit, lean), jnp.int32)
    twos = (count - 1) // 2
    donor, sink = sizes[1:1 + 2 * twos:2], sizes[2:2 + 2 * twos:2]
    margin = jnp.minimum(donor - 1, limit - sink)
    shifted = jax.random.randint(jax.random.fold_in(stream_key, 1), (twos,), 0, 1 << 20) % (margin + 1)
    sizes = sizes.at[1:1 + 2 * twos:2].set(donor - shifted).at[2:2 + 2 * twos:2].set(sink + shifted)
    return sizes[jax.random.permutation(jax.random.fold_in(stream_key, 2), count)]


def noise(rng, shape, width, reach, cuts=(), kind=jnp.bfloat16):
    entries = jax.random.normal(rng, shape, jnp.float32) * width
    if len(cuts) > 0:
        entries = levels(rng, shape, cuts, -0.22, 0.18) * entries
    return jnp.clip(entries, min=-reach, max=reach).astype(kind)


def setup_inputs(seed: int = 0) -> dict:
    key_list = jax.random.split(jax.random.key(seed), 8)
    return {
        "item_ids": draw_item_ids(jax.random.fold_in(key_list[7], 71), 0),
        "lengths": jax.vmap(lambda own: uneven(own, SEQ_DEV, TOK_DEV, MOST, 2))(jax.random.split(key_list[1], DEVICES)).reshape((DEVICES, SEQ_DEV)).astype(jnp.int32),
        "item_table": noise(key_list[2], (ROWS, D), 1.0, 6.0, ((0, 64),)),
        "admitted": place_ends((jax.random.randint(key_list[3], (ROWS,), 0, 4) < 3).astype(jnp.int32), jax.random.fold_in(key_list[3], 1), 0, 1),
        "input_weight": noise(key_list[4], (D, 4 * WIDTH), D ** -0.5, 0.1875),
        "output_weight": noise(key_list[5], (WIDTH, D), WIDTH ** -0.5, 0.25),
        "out_grad": noise(key_list[6], (TOKENS, D), 1.0, 6.0, ((0, 768),)),
    }


epsilon = 1e-05

def silu_slope(argument):
    logistic = jax.nn.sigmoid(argument)
    return logistic * (1.0 + argument * (1.0 - logistic))

def layer_norm(inputs):
    centre = inputs - lax.optimization_barrier(jnp.mean(inputs, -1, keepdims=True))
    inverse = lax.rsqrt(lax.optimization_barrier(jnp.mean(centre * centre, -1, keepdims=True)) + epsilon)
    return (centre * inverse, inverse)

def norm_back(upstream, normed, inverse):
    return inverse * (upstream - lax.optimization_barrier(jnp.mean(upstream, -1, keepdims=True)) - normed * lax.optimization_barrier(jnp.mean(upstream * normed, -1, keepdims=True)))

def contract(pattern, left_side, right_side):
    return jnp.einsum(pattern, left_side.astype(jnp.float32), right_side.astype(jnp.float32))

def contract_first(left_side, right_side):
    return lax.dot_general(left_side, right_side, (((0,), (0,)), ((), ())), preferred_element_type=jnp.float32)

def contract_last(left_side, right_side):
    return lax.dot_general(left_side, right_side, (((1,), (1,)), ((), ())), preferred_element_type=jnp.float32)

def local_layer(fetched, admit_flags, out_grad, seq_lengths, input_weight, output_weight):
    token_count = fetched.shape[0]
    feature_width = output_weight.shape[0]
    head_size = feature_width // HEADS
    positions = jnp.arange(token_count, dtype=jnp.int32)
    seq_ends = jnp.cumsum(seq_lengths).astype(jnp.int32)
    segment = lax.optimization_barrier(jnp.sum((positions[:, None] >= seq_ends[None, :]).astype(jnp.int32), axis=1))
    visible = (segment[:, None] == segment[None, :]) & (positions[None, :] <= positions[:, None])
    fetched_wide = fetched.astype(jnp.float32)
    normed, input_scale = layer_norm(fetched_wide)
    projected = jnp.dot(normed.astype(jnp.bfloat16), input_weight, preferred_element_type=jnp.float32)
    activated = jax.nn.silu(projected).astype(jnp.bfloat16)
    gating = activated[:, :feature_width]
    values = activated[:, feature_width:2 * feature_width].reshape(token_count, HEADS, head_size)
    queries = activated[:, 2 * feature_width:3 * feature_width].reshape(token_count, HEADS, head_size)
    keys_part = activated[:, 3 * feature_width:].reshape(token_count, HEADS, head_size)
    scores = contract('ihd,jhd->hij', queries, keys_part)
    weights = jnp.where(visible[None], jax.nn.silu(scores) / MOST, 0.0).astype(jnp.bfloat16)
    attended = contract('hij,jhd->ihd', weights, values).reshape(token_count, feature_width)
    head_norm, head_scale = layer_norm(attended)
    mixed_out = (head_norm * gating.astype(jnp.float32)).astype(jnp.bfloat16)
    layer_out = (fetched_wide + jnp.dot(mixed_out, output_weight, preferred_element_type=jnp.float32)).astype(jnp.bfloat16)
    weight_term = contract_first(mixed_out, out_grad)
    grad_mixed = contract_last(out_grad, output_weight)
    grad_attended = norm_back(grad_mixed * gating.astype(jnp.float32), head_norm, head_scale).astype(jnp.bfloat16)
    grad_attended = grad_attended.reshape(token_count, HEADS, head_size)
    grad_weights = contract('ihd,jhd->hij', grad_attended, values)
    grad_values = contract('hij,ihd->jhd', weights, grad_attended).reshape(token_count, feature_width)
    grad_scores = jnp.where(visible[None], grad_weights * silu_slope(scores) / MOST, 0.0).astype(jnp.bfloat16)
    grad_queries = contract('hij,jhd->ihd', grad_scores, keys_part).reshape(token_count, feature_width)
    grad_keys = contract('hij,ihd->jhd', grad_scores, queries).reshape(token_count, feature_width)
    grad_projected = jnp.concatenate([grad_mixed * head_norm, grad_values, grad_queries, grad_keys], axis=1)
    grad_projected = (grad_projected * silu_slope(projected)).astype(jnp.bfloat16)
    grad_normed = contract_last(grad_projected, input_weight)
    embed_grad = admit_flags[:, None] * (norm_back(grad_normed, normed, input_scale) + out_grad.astype(jnp.float32))
    return (layer_out, embed_grad, weight_term)

def reference(item_ids, lengths, item_table, admitted, input_weight, output_weight, out_grad):
    admit_flags = admitted[item_ids]
    fetched = item_table[item_ids] * admit_flags[:, None].astype(jnp.bfloat16)
    blocks = lengths.shape[0]
    token_count = item_ids.shape[0] // blocks
    features = item_table.shape[1]
    fetched = fetched.reshape(blocks, token_count, features)
    flag_blocks = admit_flags.astype(jnp.float32).reshape(blocks, token_count)
    grad_blocks = out_grad.reshape(blocks, token_count, features)

    def accumulate(running, pieces):
        block_rows, block_flags, block_grad, block_lengths = pieces
        layer_out, embed_grad, weight_term = local_layer(block_rows, block_flags, block_grad, block_lengths, input_weight, output_weight)
        return (running + weight_term, (layer_out, embed_grad))
    initial = jnp.zeros((output_weight.shape[0], features), jnp.float32)
    running, (layer_out, embed_grad) = lax.scan(accumulate, initial, (fetched, flag_blocks, grad_blocks, lengths))
    factor = 1.0 / math.sqrt(item_ids.shape[0])
    return (layer_out.reshape(-1, features), embed_grad.reshape(-1, features), running * factor)
```

```python
import functools
import math

import jax
import jax.numpy as jnp
from jax import lax
from jax.experimental import pallas as pl
from jax.experimental.pallas import tpu as pltpu
from jax.sharding import PartitionSpec as P

HEADS = 4
MOST = 128
CAP = 8
NX = 4
EPS = 1e-05
F32 = jnp.float32
BF16 = jnp.bfloat16
MESH = pl.DeviceIdType.MESH


def sigmoid(v):
    return 0.5 * jnp.tanh(0.5 * v) + 0.5


def mm(a, b, dims):
    return lax.dot_general(a, b, (dims, ((), ())), preferred_element_type=F32)


def iota(shape, dim):
    return lax.broadcasted_iota(jnp.int32, shape, dim)


def wait_bytes(ref, sem):
    pltpu.make_async_copy(ref, ref, sem).wait()


def kernel(
    nz, ns,
    ids_ref, len_ref, adm_ref, table_hbm, win_hbm, wout_hbm, og_hbm,
    lo_hbm, eg_hbm, wg_hbm,
    table_v, win_v, wout_v, og_v,
    req_s, req_r, flg_s, flg_r, rows_s, rows_r,
    perm, fet_v, nrm_f, nrm_b, proj, act, vism, sco, wts,
    att, hnorm, mix, gmix, gatt, gproj,
    wt_f, w1_s, w1_r, w2_s, w2_r, w3_s, w3_r, a2, a3, a4, r4, o4,
    lo_v, eg_v, wg_v,
    ld_sem, st_sem, ss, rs, rs1,
):
    ny = ns // (2 * NX)
    row = 2 * NX
    T, D = og_v.shape
    W = wout_v.shape[0]
    R = table_v.shape[0]
    H = D // 2
    hd = W // HEADS
    z = lax.axis_index("dp")
    me = lax.axis_index("table")
    core = me % 2
    x = (me // 2) % NX
    y = me // row

    bar = pltpu.get_barrier_semaphore()

    def sig_t(k, c):
        pl.semaphore_signal(bar, 1, device_id={"table": (me + k) % ns}, device_id_type=MESH)
        return c

    def sig_z(k, c):
        pl.semaphore_signal(bar, 1, device_id={"dp": (z + k) % nz}, device_id_type=MESH)
        return c

    lax.fori_loop(1, ns, sig_t, 0)
    lax.fori_loop(1, nz, sig_z, 0)

    loads = [
        pltpu.make_async_copy(table_hbm, table_v, ld_sem.at[0]),
        pltpu.make_async_copy(wout_hbm, wout_v, ld_sem.at[1]),
        pltpu.make_async_copy(og_hbm, og_v, ld_sem.at[2]),
        pltpu.make_async_copy(win_hbm, win_v, ld_sem.at[3]),
    ]
    for c in loads:
        c.start()

    ids_row = ids_ref[...]
    own_row = ids_row >> (R.bit_length() - 1)
    ri = iota((T, T), 0)
    ci = iota((T, T), 1)
    ids_col = jnp.sum(
        jnp.where(ri == ci, jnp.broadcast_to(ids_row.astype(F32), (T, T)), 0.0), axis=1, keepdims=True
    ).astype(jnp.int32)
    own_col = ids_col >> (R.bit_length() - 1)
    loc_col = ids_col & (R - 1)
    before = (own_col == own_row) & (ci < ri)
    rank_col = jnp.sum(jnp.where(before, 1.0, 0.0), axis=1, keepdims=True).astype(jnp.int32)
    owner_hot = jnp.where(iota((ns, T), 0) == own_row, 1.0, 0.0).astype(BF16)
    at_rank = iota((T, 128), 1) == rank_col
    hi = jnp.where(at_rank, (loc_col >> 5).astype(F32), 0.0).astype(BF16)
    lo = jnp.where(at_rank, (loc_col & 31).astype(F32), 0.0).astype(BF16)
    req = mm(owner_hot, hi, ((1,), (0,))) * 32.0 + mm(owner_hot, lo, ((1,), (0,)))
    for s in range(ns):
        req_s[s] = req[s : s + 1, :]
    req_r[me] = req_s[me]

    pl.semaphore_wait(bar, ns - 1 + nz - 1)

    def send_req(k, c):
        peer = (me + k) % ns
        pltpu.make_async_remote_copy(
            req_s.at[peer], req_r.at[me], ss.at[0], rs.at[0], device_id={"table": peer}, device_id_type=MESH
        ).start()
        return c

    lax.fori_loop(1, ns, send_req, 0)

    slot = own_col * (2 * CAP) + rank_col
    pi = iota((T, ns * 2 * CAP), 1)
    perm[pl.ds(0, T)] = jnp.where(pi == slot, 1.0, 0.0).astype(BF16)
    perm[pl.ds(T, T)] = jnp.where(pi == slot + CAP, 1.0, 0.0).astype(BF16)

    l0 = len_ref[0, 0]
    l1 = l0 + len_ref[0, 1]
    l2 = l1 + len_ref[0, 2]

    def segment(pos):
        one = jnp.where(pos >= l0, 1, 0)
        two = jnp.where(pos >= l1, 1, 0)
        return one + two + jnp.where(pos >= l2, 1, 0)

    vism[...] = jnp.where((segment(ri) == segment(ci)) & (ci <= ri), 1.0 / MOST, 0.0)

    loads[0].wait()
    adm = adm_ref[...].astype(F32)
    wait_bytes(req_r.at[pl.ds(0, ns - 1)], rs.at[0])
    half = max(ny // 2, 1)
    ones = jnp.ones((R, 128), BF16)
    for part in range(ny // half):
        hot = []
        for j in range(half):
            yy = (y + ny // 4 + part * half + j) % ny
            r = jnp.broadcast_to(req_r[pl.ds(yy * row, row)], (row, CAP, 128))
            r = jnp.where(iota((row, CAP, 128), 1) == iota((row, CAP, 128), 2), r, 0.0)
            r = jnp.sum(r, axis=2, keepdims=True).reshape(row * CAP, 1).astype(jnp.int32)
            hot.append(jnp.where(iota((row * CAP, R), 1) == r, adm, 0.0).astype(BF16))
        hot = jnp.concatenate(hot, axis=0)
        got = mm(hot, table_v[...], ((1,), (0,)))
        got = jnp.concatenate(
            [got[:, :H].reshape(half * row, CAP, H), got[:, H:].reshape(half * row, CAP, H)], axis=1
        ).astype(BF16)
        flg = mm(hot, ones, ((1,), (0,))).reshape(half * row, CAP, 128)
        flg = jnp.where(iota(flg.shape, 1) == iota(flg.shape, 2), flg, 0.0)
        flg = jnp.sum(flg, axis=1, keepdims=True)
        for j in range(half):
            yy = (y + ny // 4 + part * half + j) % ny
            rows_s[pl.ds(yy * row, row)] = got[j * row : (j + 1) * row]
            flg_s[pl.ds(yy * row, row)] = flg[j * row : (j + 1) * row]

        def send_rows(k, c):
            yy = (y + ny // 4 + part * half + k // row) % ny
            peer = yy * row + (me + k) % row

            @pl.when(peer != me)
            def _():
                pltpu.make_async_remote_copy(
                    rows_s.at[peer], rows_r.at[me], ss.at[1], rs.at[1],
                    device_id={"table": peer}, device_id_type=MESH,
                ).start()

            return c

        lax.fori_loop(0, half * row, send_rows, 0)

    def send_flg(k, c):
        peer = (me + k) % ns
        pltpu.make_async_remote_copy(
            flg_s.at[peer], flg_r.at[me], ss.at[2], rs.at[2], device_id={"table": peer}, device_id_type=MESH
        ).start()
        return c

    lax.fori_loop(1, ns, send_flg, 0)
    rows_r[me] = rows_s[me]
    flg_r[me] = flg_s[me]

    loads[1].wait()
    loads[2].wait()
    gmix[...] = mm(og_v[...], wout_v[...], ((1,), (1,)))
    loads[3].wait()

    wait_bytes(rows_r.at[pl.ds(0, ns - 1)], rs.at[1])
    got = mm(perm[...], rows_r[...].reshape(ns * 2 * CAP, H), ((1,), (0,)))
    fet = jnp.concatenate([got[:T], got[T:]], axis=1)
    fet_v[...] = fet
    cen = fet - jnp.sum(fet, axis=1, keepdims=True) * (1.0 / D)
    inv = lax.rsqrt(jnp.sum(cen * cen, axis=1, keepdims=True) * (1.0 / D) + EPS)
    nrm = cen * inv
    nrm_f[...] = nrm
    nrm_b[...] = nrm.astype(BF16)

    wide = min(256, 4 * W)
    for n in range(4 * W // wide):
        cols = slice(n * wide, (n + 1) * wide)
        p = mm(nrm_b[...], win_v[:, cols], ((1,), (0,)))
        proj[:, cols] = p
        act[:, cols] = (p * sigmoid(p)).astype(BF16)

    for h in range(HEADS):
        v = act[:, W + h * hd : W + (h + 1) * hd]
        q = act[:, 2 * W + h * hd : 2 * W + (h + 1) * hd]
        k = act[:, 3 * W + h * hd : 3 * W + (h + 1) * hd]
        s = mm(q, k, ((1,), (1,)))
        sco[h] = s
        w = (s * sigmoid(s) * vism[...]).astype(BF16)
        wts[h] = w
        att[:, h * hd : (h + 1) * hd] = mm(w, v, ((1,), (0,)))

    a = att[...]
    a = a - jnp.sum(a, axis=1, keepdims=True) * (1.0 / W)
    hscale = lax.rsqrt(jnp.sum(a * a, axis=1, keepdims=True) * (1.0 / W) + EPS)
    hn = a * hscale
    hnorm[...] = hn
    mix[...] = (hn * act[:, :W].astype(F32)).astype(BF16)

    factor = 1.0 / math.sqrt(T * nz * ns)
    for c in range(2):
        wt = mm(mix[...], og_v[:, c * H : (c + 1) * H], ((0,), (0,))) * factor
        wt = wt.reshape(ny, NX, 2, 8, H)
        for xx in range(NX):
            for cc in range(2):
                wt_f[cc, xx, :, c * 8 : (c + 1) * 8, :] = wt[:, xx, cc]

    partner = me + 1 - 2 * core
    pair = []
    for i in range(NX):
        xx = (x + NX // 2 + i) % NX
        w1_s[xx] = wt_f[1 - core, xx].astype(BF16)
        c = pltpu.make_async_remote_copy(
            w1_s.at[xx], w1_r.at[xx], ss.at[3], rs1.at[xx], device_id={"table": partner}, device_id_type=MESH
        )
        c.start()
        pair.append(c)

    lo_v[...] = (fet_v[...] + mm(mix[...], wout_v[...], ((1,), (0,)))).astype(BF16)
    put_lo = pltpu.make_async_copy(lo_v, lo_hbm, st_sem.at[0])
    put_lo.start()

    for i in range(NX):
        xx = (x + NX // 2 + i) % NX
        pltpu.make_async_copy(w1_r.at[xx], w1_r.at[xx], rs1.at[xx]).wait()
        total = wt_f[core, xx] + w1_r[xx].astype(F32)
        w2_s[xx] = total.astype(BF16)
        if i == NX - NX // 2:
            a2[...] = total
        else:
            pltpu.make_async_remote_copy(
                w2_s.at[xx], w2_r.at[x], ss.at[4], rs.at[3],
                device_id={"table": (y * NX + xx) * 2 + core}, device_id_type=MESH,
            ).start()

    g = gmix[...] * act[:, :W].astype(F32)
    hn = hnorm[...]
    g = g - jnp.sum(g, axis=1, keepdims=True) * (1.0 / W) - hn * (jnp.sum(g * hn, axis=1, keepdims=True) * (1.0 / W))
    gatt[...] = (hscale * g).astype(BF16)

    def through_silu(grad, at):
        p = proj[:, at : at + grad.shape[1]]
        s = sigmoid(p)
        gproj[:, at : at + grad.shape[1]] = (grad * (s * (1.0 + p * (1.0 - s)))).astype(BF16)

    through_silu(gmix[...] * hn, 0)

    wait_bytes(w2_r.at[pl.ds(0, NX - 1)], rs.at[3])
    w2_r[x] = jnp.zeros(w2_r.shape[1:], BF16)
    total = a2[...]
    for i in range(NX):
        total = total + w2_r[i].astype(F32)
    w3_s[...] = total.astype(BF16)
    a3[...] = total

    def send_y(k, c):
        yy = (y + k) % ny
        pltpu.make_async_remote_copy(
            w3_s.at[yy], w3_r.at[y], ss.at[5], rs.at[4],
            device_id={"table": (yy * NX + x) * 2 + core}, device_id_type=MESH,
        ).start()
        return c

    lax.fori_loop(1, ny, send_y, 0)

    for h in range(HEADS):
        v = act[:, W + h * hd : W + (h + 1) * hd]
        q = act[:, 2 * W + h * hd : 2 * W + (h + 1) * hd]
        k = act[:, 3 * W + h * hd : 3 * W + (h + 1) * hd]
        ga = gatt[:, h * hd : (h + 1) * hd]
        gw = mm(ga, v, ((1,), (1,)))
        gv = mm(wts[h], ga, ((0,), (0,)))
        sv = sco[h]
        s = sigmoid(sv)
        gs = (gw * (s * (1.0 + sv * (1.0 - s))) * vism[...]).astype(BF16)
        gq = mm(gs, k, ((1,), (0,)))
        gk = mm(gs, q, ((0,), (0,)))
        through_silu(gv, W + h * hd)
        through_silu(gq, 2 * W + h * hd)
        through_silu(gk, 3 * W + h * hd)

    wait_bytes(w3_r.at[pl.ds(0, ny - 1)], rs.at[4])
    w3_r[y] = jnp.zeros(w3_r.shape[1:], BF16)
    total = a3[y]
    for i in range(ny):
        total = total + w3_r[i].astype(F32)
    nt = D // 128
    for j in range(nt):
        c, at = divmod(j, nt // 2)
        a4[j] = total[c * 8 : (c + 1) * 8, at * 128 : (at + 1) * 128]

    @pl.when(z < nt)
    def _():
        r4[z] = a4[jnp.minimum(z, nt - 1)]

    for j in range(nt):

        @pl.when(z != j)
        def _():
            pltpu.make_async_remote_copy(
                a4.at[j], r4.at[z], ss.at[6], rs.at[5], device_id={"dp": j}, device_id_type=MESH
            ).start()

    gn = mm(gproj[...], win_v[...], ((1,), (1,)))
    nrm = nrm_f[...]
    m1 = jnp.sum(gn, axis=1, keepdims=True) * (1.0 / D)
    m2 = jnp.sum(gn * nrm, axis=1, keepdims=True) * (1.0 / D)
    wait_bytes(flg_r.at[pl.ds(0, ns - 1)], rs.at[2])
    flags = jnp.concatenate([flg_r[s] for s in range(ns)], axis=0).astype(BF16)
    own_hot = jnp.where(iota((T, ns), 1) == own_col, 1.0, 0.0).astype(BF16)
    flag = mm(own_hot, flags, ((1,), (0,)))
    flag = jnp.sum(jnp.where(at_rank, flag, 0.0), axis=1, keepdims=True)
    eg_v[...] = flag * (inv * (gn - m1 - nrm * m2) + og_v[...].astype(F32))
    put_eg = pltpu.make_async_copy(eg_v, eg_hbm, st_sem.at[1])
    put_eg.start()

    @pl.when(z < nt)
    def _():
        wait_bytes(r4.at[pl.ds(0, nz - 1)], rs.at[5])
        acc = r4[0]
        for i in range(1, nz):
            acc = acc + r4[i]
        zz = jnp.minimum(z, nt - 1)
        o4[zz] = acc

        def send_o(k, c):
            pltpu.make_async_remote_copy(
                o4.at[zz], o4.at[zz], ss.at[7], rs.at[6], device_id={"dp": (z + k) % nz}, device_id_type=MESH
            ).start()
            return c

        lax.fori_loop(1, nz, send_o, 0)
        wait_bytes(o4.at[pl.ds(0, nt - 1)], rs.at[6])
        wait_bytes(a4.at[pl.ds(0, nt - 1)], ss.at[6])
        wait_bytes(r4.at[pl.ds(0, nz - 1)], ss.at[7])

    @pl.when(z >= nt)
    def _():
        wait_bytes(o4, rs.at[6])
        wait_bytes(a4, ss.at[6])

    for j in range(nt):
        wg_v[:, j * 128 : (j + 1) * 128] = o4[j]
    put_wg = pltpu.make_async_copy(wg_v, wg_hbm, st_sem.at[2])
    put_wg.start()

    wait_bytes(req_s.at[pl.ds(0, ns - 1)], ss.at[0])
    wait_bytes(rows_s.at[pl.ds(0, ns - 1)], ss.at[1])
    wait_bytes(flg_s.at[pl.ds(0, ns - 1)], ss.at[2])
    wait_bytes(w1_s, ss.at[3])
    wait_bytes(w2_s.at[pl.ds(0, NX - 1)], ss.at[4])
    wait_bytes(w3_s.at[pl.ds(0, ny - 1)], ss.at[5])
    put_lo.wait()
    put_eg.wait()
    put_wg.wait()


def on_device(nz, item_ids, lengths, item_table, admitted, input_weight, output_weight, out_grad):
    ns = lax.axis_size("table")
    ny = ns // (2 * NX)
    T = item_ids.shape[0]
    R, D = item_table.shape
    W = output_weight.shape[0]
    H = D // 2
    nt = D // 128
    V = pltpu.VMEM
    vspec = pl.BlockSpec(memory_space=pltpu.VMEM)
    hspec = pl.BlockSpec(memory_space=pl.ANY)
    scratch = [
        V((R, D), BF16), V((D, 4 * W), BF16), V((W, D), BF16), V((T, D), BF16),
        V((ns, 1, 128), F32), V((ns, 1, 128), F32), V((ns, 1, 128), F32), V((ns, 1, 128), F32),
        V((ns, 2 * CAP, H), BF16), V((ns, 2 * CAP, H), BF16),
        V((2 * T, ns * 2 * CAP), BF16), V((T, D), F32), V((T, D), F32), V((T, D), BF16),
        V((T, 4 * W), F32), V((T, 4 * W), BF16), V((T, T), F32), V((HEADS, T, T), F32), V((HEADS, T, T), BF16),
        V((T, W), F32), V((T, W), F32), V((T, W), BF16), V((T, W), F32), V((T, W), BF16), V((T, 4 * W), BF16),
        V((2, NX, ny, 16, H), F32), V((NX, ny, 16, H), BF16), V((NX, ny, 16, H), BF16),
        V((NX, ny, 16, H), BF16), V((NX, ny, 16, H), BF16), V((ny, 16, H), BF16), V((ny, 16, H), BF16),
        V((ny, 16, H), F32), V((ny, 16, H), F32), V((nt, 8, 128), F32), V((nz, 8, 128), F32), V((nt, 8, 128), F32),
        V((T, D), BF16), V((T, D), F32), V((8, D), F32),
        pltpu.SemaphoreType.DMA((4,)), pltpu.SemaphoreType.DMA((3,)),
        pltpu.SemaphoreType.DMA((8,)), pltpu.SemaphoreType.DMA((7,)), pltpu.SemaphoreType.DMA((NX,)),
    ]
    return pl.pallas_call(
        functools.partial(kernel, nz, ns),
        out_shape=(
            jax.ShapeDtypeStruct((T, D), BF16),
            jax.ShapeDtypeStruct((T, D), F32),
            jax.ShapeDtypeStruct((8, D), F32),
        ),
        in_specs=[vspec, pl.BlockSpec(memory_space=pltpu.SMEM), vspec, hspec, hspec, hspec, hspec],
        out_specs=(hspec, hspec, hspec),
        scratch_shapes=scratch,
        compiler_params=pltpu.CompilerParams(
            collective_id=0, has_side_effects=True, vmem_limit_bytes=56 * 1024 * 1024
        ),
        name="layer",
    )(
        item_ids.reshape(1, T), lengths, admitted.reshape(1, R), item_table, input_weight, output_weight, out_grad
    )


def solution(mesh):
    return jax.shard_map(
        functools.partial(on_device, mesh.shape["dp"]),
        mesh=mesh,
        in_specs=(
            P(("dp", "table")),
            P(("dp", "table"), None),
            P("table", None),
            P("table"),
            P(),
            P(),
            P(("dp", "table"), None),
        ),
        out_specs=(P(("dp", "table"), None), P(("dp", "table"), None), P("table", None)),
        check_vma=False,
    )
```

```python
import functools
import math

import jax
import jax.numpy as jnp
from jax import lax
from jax.experimental import pallas as pl
from jax.experimental.pallas import tpu as pltpu
from jax.sharding import PartitionSpec as P

HEADS = 4
MOST = 128
CAP = 8
NX = 4
EPS = 1e-05
F32 = jnp.float32
BF16 = jnp.bfloat16
MESH = pl.DeviceIdType.MESH


def sigmoid(v):
    return 0.5 * jnp.tanh(0.5 * v) + 0.5


def mm(a, b, dims):
    return lax.dot_general(a, b, (dims, ((), ())), preferred_element_type=F32)


def iota(shape, dim):
    return lax.broadcasted_iota(jnp.int32, shape, dim)


def wait_bytes(ref, sem):
    pltpu.make_async_copy(ref, ref, sem).wait()


def groups(ny):
    return [(1, 7), (4, 3), (5, 2), (6, 0)] if ny == 8 else [((k + 1) % ny,) for k in range(ny)]


def z_split(nz):
    near = 4 if nz % 4 == 0 else 1
    return near, nz // near


def kernel(
    nz, ns,
    ids_ref, len_ref, adm_ref, table_hbm, win_hbm, wout_hbm, og_hbm,
    lo_v, eg_v, wg_v,
    table_v, win_v, wout_v, og_v,
    req_s, req_r, flg_s, flg_r, rows_s, rows_r,
    perm, fet_v, nrm_f, nrm_b, proj, act, vism, sco, wts,
    att, hnorm, mix, gmix, gatt, gproj,
    wt_f, w1_s, w1_r, xa_s, xa_r, yb_s, yb_r, ya_s, ya_r, xb_s, xb_r,
    own_xa, own_ya, zr, zg,
    ld_sem, ss, rs, rs_req, rs1,
):
    ny = ns // (2 * NX)
    row = 2 * NX
    T, D = og_v.shape
    W = wout_v.shape[0]
    R = table_v.shape[0]
    H = D // 2
    HA = xa_s.shape[-1]
    hd = W // HEADS
    z = lax.axis_index("dp")
    me = lax.axis_index("table")
    core = me % 2
    x = (me // 2) % NX
    y = me // row
    near, far = z_split(nz)
    zl = z % near
    zg_me = z // near

    def copy(src, dst, i, to, sem=None):
        c = pltpu.make_async_remote_copy(
            src, dst, ss.at[i], rs.at[i] if sem is None else sem, device_id=to, device_id_type=MESH
        )
        c.start()

    bar = pltpu.get_barrier_semaphore()

    def sig_t(k, c):
        pl.semaphore_signal(bar, 1, device_id={"table": (me + k) % ns}, device_id_type=MESH)
        return c

    lax.fori_loop(3 * ns // 8, ns, sig_t, 0)
    lax.fori_loop(1, 3 * ns // 8, sig_t, 0)
    near_z = [zg_me * near + (zl + i) % near for i in range(1, near)]
    far_z = [((zg_me + i) % far) * near + zl for i in range(1, far)]
    for to in near_z + far_z:
        pl.semaphore_signal(bar, 1, device_id={"dp": to}, device_id_type=MESH)

    loads = [
        pltpu.make_async_copy(table_hbm, table_v, ld_sem.at[0]),
        pltpu.make_async_copy(wout_hbm, wout_v, ld_sem.at[1]),
        pltpu.make_async_copy(og_hbm, og_v, ld_sem.at[2]),
        pltpu.make_async_copy(win_hbm, win_v, ld_sem.at[3]),
    ]
    loads[0].start()

    ids_row = ids_ref[...]
    own_row = ids_row >> (R.bit_length() - 1)
    ri = iota((T, T), 0)
    ci = iota((T, T), 1)
    ids_col = jnp.sum(
        jnp.where(ri == ci, jnp.broadcast_to(ids_row.astype(F32), (T, T)), 0.0), axis=1, keepdims=True
    ).astype(jnp.int32)
    own_col = ids_col >> (R.bit_length() - 1)
    loc_col = ids_col & (R - 1)
    before = (own_col == own_row) & (ci < ri)
    rank_col = jnp.sum(jnp.where(before, 1.0, 0.0), axis=1, keepdims=True).astype(jnp.int32)
    owner_hot = jnp.where(iota((ns, T), 0) == own_row, 1.0, 0.0).astype(BF16)
    at_rank = iota((T, 128), 1) == rank_col
    hi = jnp.where(at_rank, (loc_col >> 5).astype(F32), 0.0).astype(BF16)
    lo = jnp.where(at_rank, (loc_col & 31).astype(F32), 0.0).astype(BF16)
    req = mm(owner_hot, hi, ((1,), (0,))) * 32.0 + mm(owner_hot, lo, ((1,), (0,)))
    for s in range(ns):
        req_s[s] = req[s : s + 1, :]
    req_r[me] = req_s[me]

    pl.semaphore_wait(bar, ns - 1 + len(near_z) + len(far_z))

    for gi, dys in enumerate(groups(ny)):
        for dy in dys:

            def send_req(k, c):
                peer = ((y + ny - dy) % ny) * row + (me + k) % row
                copy(req_s.at[peer], req_r.at[me], 0, {"table": peer}, rs_req.at[gi])
                return c

            lax.fori_loop(0 if dy else 1, row, send_req, 0)

    for c in loads[1:]:
        c.start()

    slot = own_col * (2 * CAP) + rank_col
    pi = iota((T, ns * 2 * CAP), 1)
    perm[pl.ds(0, T)] = jnp.where(pi == slot, 1.0, 0.0).astype(BF16)
    perm[pl.ds(T, T)] = jnp.where(pi == slot + CAP, 1.0, 0.0).astype(BF16)

    l0 = len_ref[0, 0]
    l1 = l0 + len_ref[0, 1]
    l2 = l1 + len_ref[0, 2]

    def segment(pos):
        one = jnp.where(pos >= l0, 1, 0)
        two = jnp.where(pos >= l1, 1, 0)
        return one + two + jnp.where(pos >= l2, 1, 0)

    vism[...] = jnp.where((segment(ri) == segment(ci)) & (ci <= ri), 1.0 / MOST, 0.0)

    loads[0].wait()
    adm = adm_ref[...].astype(F32)
    ones = jnp.ones((R, 128), BF16)
    for gi, dys in enumerate(groups(ny)):
        n = len(dys)
        wait_bytes(req_r.at[pl.ds(0, n * row - (0 in dys))], rs_req.at[gi])
        hot = []
        for dy in dys:
            yy = (y + dy) % ny
            r = jnp.broadcast_to(req_r[pl.ds(yy * row, row)], (row, CAP, 128))
            r = jnp.where(iota((row, CAP, 128), 1) == iota((row, CAP, 128), 2), r, 0.0)
            r = jnp.sum(r, axis=2, keepdims=True).reshape(row * CAP, 1).astype(jnp.int32)
            hot.append(jnp.where(iota((row * CAP, R), 1) == r, adm, 0.0).astype(BF16))
        hot = jnp.concatenate(hot, axis=0)
        got = mm(hot, table_v[...], ((1,), (0,)))
        got = jnp.concatenate(
            [got[:, :H].reshape(n * row, CAP, H), got[:, H:].reshape(n * row, CAP, H)], axis=1
        ).astype(BF16)
        for j, dy in enumerate(dys):
            yy = (y + dy) % ny
            rows_s[pl.ds(yy * row, row)] = got[j * row : (j + 1) * row]

        for dy in dys:

            def send_rows(k, c):
                peer = ((y + dy) % ny) * row + (me + k) % row
                copy(rows_s.at[peer], rows_r.at[me], 1, {"table": peer})
                return c

            lax.fori_loop(0 if dy else 1, row, send_rows, 0)
        flg = mm(hot, ones, ((1,), (0,))).reshape(n * row, CAP, 128)
        flg = jnp.where(iota(flg.shape, 1) == iota(flg.shape, 2), flg, 0.0)
        flg = jnp.sum(flg, axis=1, keepdims=True)
        for j, dy in enumerate(dys):
            yy = (y + dy) % ny
            flg_s[pl.ds(yy * row, row)] = flg[j * row : (j + 1) * row]

    def send_flg(k, c):
        peer = (me + k) % ns
        copy(flg_s.at[peer], flg_r.at[me], 2, {"table": peer})
        return c

    lax.fori_loop(1, ns, send_flg, 0)
    rows_r[me] = rows_s[me]
    flg_r[me] = flg_s[me]

    loads[1].wait()
    loads[2].wait()
    gmix[...] = mm(og_v[...], wout_v[...], ((1,), (1,)))
    loads[3].wait()

    wait_bytes(rows_r.at[pl.ds(0, ns - 1)], rs.at[1])
    got = mm(perm[...], rows_r[...].reshape(ns * 2 * CAP, H), ((1,), (0,)))
    fet = jnp.concatenate([got[:T], got[T:]], axis=1)
    fet_v[...] = fet
    cen = fet - jnp.sum(fet, axis=1, keepdims=True) * (1.0 / D)
    inv = lax.rsqrt(jnp.sum(cen * cen, axis=1, keepdims=True) * (1.0 / D) + EPS)
    nrm = cen * inv
    nrm_f[...] = nrm
    nrm_b[...] = nrm.astype(BF16)

    wide = min(256, 4 * W)
    for n in range(4 * W // wide):
        cols = slice(n * wide, (n + 1) * wide)
        p = mm(nrm_b[...], win_v[:, cols], ((1,), (0,)))
        proj[:, cols] = p
        act[:, cols] = (p * sigmoid(p)).astype(BF16)

    for h in range(HEADS):
        v = act[:, W + h * hd : W + (h + 1) * hd]
        q = act[:, 2 * W + h * hd : 2 * W + (h + 1) * hd]
        k = act[:, 3 * W + h * hd : 3 * W + (h + 1) * hd]
        s = mm(q, k, ((1,), (1,)))
        sco[h] = s
        w = (s * sigmoid(s) * vism[...]).astype(BF16)
        wts[h] = w
        att[:, h * hd : (h + 1) * hd] = mm(w, v, ((1,), (0,)))

    a = att[...]
    a = a - jnp.sum(a, axis=1, keepdims=True) * (1.0 / W)
    hscale = lax.rsqrt(jnp.sum(a * a, axis=1, keepdims=True) * (1.0 / W) + EPS)
    hn = a * hscale
    hnorm[...] = hn
    mix[...] = (hn * act[:, :W].astype(F32)).astype(BF16)

    factor = 1.0 / math.sqrt(T * nz * ns)
    for c in range(2):
        wt = mm(mix[...], og_v[:, c * H : (c + 1) * H], ((0,), (0,))) * factor
        wt = wt.reshape(ny, NX, 2, 8, H)
        for xx in range(NX):
            for cc in range(2):
                wt_f[cc, xx, :, c * 8 : (c + 1) * 8, :] = wt[:, xx, cc]

    partner = me + 1 - 2 * core
    for i in range(NX):
        xx = (x + NX // 2 + i) % NX
        w1_s[xx] = wt_f[1 - core, xx].astype(BF16)
        copy(w1_s.at[xx], w1_r.at[xx], 3, {"table": partner}, rs1.at[xx])

    lo_v[...] = (fet_v[...] + mm(mix[...], wout_v[...], ((1,), (0,)))).astype(BF16)

    for i in range(NX):
        xx = (x + NX // 2 + i) % NX
        wait_bytes(w1_r.at[xx], rs1.at[xx])
        total = wt_f[core, xx] + w1_r[xx].astype(F32)
        yb_s[:, xx] = total[..., HA:].astype(BF16)
        if i == NX - NX // 2:
            own_xa[...] = total[..., :HA]
        else:
            xa_s[xx] = total[..., :HA].astype(BF16)
            copy(xa_s.at[xx], xa_r.at[x], 4, {"table": (y * NX + xx) * 2 + core})
    xa_r[x] = jnp.zeros(xa_r.shape[1:], BF16)

    def send_yb(k, c):
        yy = (y + k) % ny
        copy(yb_s.at[yy], yb_r.at[y], 5, {"table": (yy * NX + x) * 2 + core})
        return c

    lax.fori_loop(1, ny, send_yb, 0)
    yb_r[y] = yb_s[y]

    g = gmix[...] * act[:, :W].astype(F32)
    hn = hnorm[...]
    g = g - jnp.sum(g, axis=1, keepdims=True) * (1.0 / W) - hn * (jnp.sum(g * hn, axis=1, keepdims=True) * (1.0 / W))
    gatt[...] = (hscale * g).astype(BF16)

    def through_silu(grad, at):
        p = proj[:, at : at + grad.shape[1]]
        s = sigmoid(p)
        gproj[:, at : at + grad.shape[1]] = (grad * (s * (1.0 + p * (1.0 - s)))).astype(BF16)

    through_silu(gmix[...] * hn, 0)
    for h in range(HEADS):
        v = act[:, W + h * hd : W + (h + 1) * hd]
        q = act[:, 2 * W + h * hd : 2 * W + (h + 1) * hd]
        k = act[:, 3 * W + h * hd : 3 * W + (h + 1) * hd]
        ga = gatt[:, h * hd : (h + 1) * hd]
        gw = mm(ga, v, ((1,), (1,)))
        gv = mm(wts[h], ga, ((0,), (0,)))
        sv = sco[h]
        s = sigmoid(sv)
        gs = (gw * (s * (1.0 + sv * (1.0 - s))) * vism[...]).astype(BF16)
        gq = mm(gs, k, ((1,), (0,)))
        gk = mm(gs, q, ((0,), (0,)))
        through_silu(gv, W + h * hd)
        through_silu(gq, 2 * W + h * hd)
        through_silu(gk, 3 * W + h * hd)

    wait_bytes(xa_r.at[pl.ds(0, NX - 1)], rs.at[4])
    total = own_xa[...]
    for i in range(NX):
        total = total + xa_r[i].astype(F32)
    ya_s[...] = total.astype(BF16)
    own_ya[...] = total

    def send_ya(k, c):
        yy = (y + k) % ny
        copy(ya_s.at[yy], ya_r.at[y], 6, {"table": (yy * NX + x) * 2 + core})
        return c

    lax.fori_loop(1, ny, send_ya, 0)
    ya_r[y] = jnp.zeros(ya_r.shape[1:], BF16)
    wait_bytes(yb_r.at[pl.ds(0, ny - 1)], rs.at[5])
    total = yb_r[0].astype(F32)
    for i in range(1, ny):
        total = total + yb_r[i].astype(F32)
    xb_s[...] = total.astype(BF16)
    for i in range(1, NX):
        xx = (x + i) % NX
        copy(xb_s.at[xx], xb_r.at[x], 7, {"table": (y * NX + xx) * 2 + core})
    xb_r[x] = xb_s[x]

    gn = mm(gproj[...], win_v[...], ((1,), (1,)))
    nrm = nrm_f[...]
    m1 = jnp.sum(gn, axis=1, keepdims=True) * (1.0 / D)
    m2 = jnp.sum(gn * nrm, axis=1, keepdims=True) * (1.0 / D)
    wait_bytes(flg_r.at[pl.ds(0, ns - 1)], rs.at[2])
    flags = jnp.concatenate([flg_r[s] for s in range(ns)], axis=0).astype(BF16)
    own_hot = jnp.where(iota((T, ns), 1) == own_col, 1.0, 0.0).astype(BF16)
    flag = mm(own_hot, flags, ((1,), (0,)))
    flag = jnp.sum(jnp.where(at_rank, flag, 0.0), axis=1, keepdims=True)
    eg_v[...] = flag * (inv * (gn - m1 - nrm * m2) + og_v[...].astype(F32))

    wait_bytes(ya_r.at[pl.ds(0, ny - 1)], rs.at[6])
    total = own_ya[y]
    for i in range(ny):
        total = total + ya_r[i].astype(F32)
    zr[zl, :, pl.ds(0, HA)] = total.astype(BF16)
    wait_bytes(xb_r.at[pl.ds(0, NX - 1)], rs.at[7])
    total = xb_r[0].astype(F32)
    for i in range(1, NX):
        total = total + xb_r[i].astype(F32)
    zr[zl, :, pl.ds(HA, H - HA)] = total.astype(BF16)
    for to in near_z:
        copy(zr.at[zl], zr.at[zl], 8, {"dp": to})
    if near > 1:
        wait_bytes(zr.at[pl.ds(0, near - 1)], rs.at[8])
    total = zr[0].astype(F32)
    for i in range(1, near):
        total = total + zr[i].astype(F32)
    zg[zg_me] = total.astype(BF16)
    for to in far_z:
        copy(zg.at[zg_me], zg.at[zg_me], 9, {"dp": to})
    if far > 1:
        wait_bytes(zg.at[pl.ds(0, far - 1)], rs.at[9])
    total = zg[0].astype(F32)
    for i in range(1, far):
        total = total + zg[i].astype(F32)
    wg_v[:, :H] = total[:8]
    wg_v[:, H:] = total[8:]

    wait_bytes(req_s.at[pl.ds(0, ns - 1)], ss.at[0])
    wait_bytes(rows_s.at[pl.ds(0, ns - 1)], ss.at[1])
    wait_bytes(flg_s.at[pl.ds(0, ns - 1)], ss.at[2])
    wait_bytes(w1_s, ss.at[3])
    wait_bytes(xa_s.at[pl.ds(0, NX - 1)], ss.at[4])
    wait_bytes(yb_s.at[pl.ds(0, ny - 1)], ss.at[5])
    wait_bytes(ya_s.at[pl.ds(0, ny - 1)], ss.at[6])
    wait_bytes(xb_s.at[pl.ds(0, NX - 1)], ss.at[7])
    if near > 1:
        wait_bytes(zr.at[pl.ds(0, near - 1)], ss.at[8])
    if far > 1:
        wait_bytes(zg.at[pl.ds(0, far - 1)], ss.at[9])


def write_out(lo, eg, wg, lo_out, eg_out, wg_out, sems):
    copies = [
        pltpu.make_async_copy(a, b, sems.at[i])
        for i, (a, b) in enumerate(((eg, eg_out), (lo, lo_out), (wg, wg_out)))
    ]
    for c in copies:
        c.start()
    for c in copies:
        c.wait()


def on_device(nz, item_ids, lengths, item_table, admitted, input_weight, output_weight, out_grad):
    ns = lax.axis_size("table")
    ny = ns // (2 * NX)
    T = item_ids.shape[0]
    R, D = item_table.shape
    W = output_weight.shape[0]
    H = D // 2
    HA = H - H // 4 if H >= 512 else H // 2
    near, far = z_split(nz)
    V = pltpu.VMEM
    vspec = pl.BlockSpec(memory_space=pltpu.VMEM)
    hspec = pl.BlockSpec(memory_space=pltpu.HBM)
    scratch = [
        V((R, D), BF16), V((D, 4 * W), BF16), V((W, D), BF16), V((T, D), BF16),
        V((ns, 1, 128), F32), V((ns, 1, 128), F32), V((ns, 1, 128), F32), V((ns, 1, 128), F32),
        V((ns, 2 * CAP, H), BF16), V((ns, 2 * CAP, H), BF16),
        V((2 * T, ns * 2 * CAP), BF16), V((T, D), F32), V((T, D), F32), V((T, D), BF16),
        V((T, 4 * W), F32), V((T, 4 * W), BF16), V((T, T), F32), V((HEADS, T, T), F32), V((HEADS, T, T), BF16),
        V((T, W), F32), V((T, W), F32), V((T, W), BF16), V((T, W), F32), V((T, W), BF16), V((T, 4 * W), BF16),
        V((2, NX, ny, 16, H), F32), V((NX, ny, 16, H), BF16), V((NX, ny, 16, H), BF16),
        V((NX, ny, 16, HA), BF16), V((NX, ny, 16, HA), BF16),
        V((ny, NX, 16, H - HA), BF16), V((ny, NX, 16, H - HA), BF16),
        V((ny, 16, HA), BF16), V((ny, 16, HA), BF16),
        V((NX, 16, H - HA), BF16), V((NX, 16, H - HA), BF16),
        V((ny, 16, HA), F32), V((ny, 16, HA), F32), V((near, 16, H), BF16), V((far, 16, H), BF16),
        pltpu.SemaphoreType.DMA((4,)),
        pltpu.SemaphoreType.DMA((10,)), pltpu.SemaphoreType.DMA((10,)),
        pltpu.SemaphoreType.DMA((len(groups(ny)),)), pltpu.SemaphoreType.DMA((NX,)),
    ]
    results = pl.pallas_call(
        functools.partial(kernel, nz, ns),
        out_shape=(V((T, D), BF16), V((T, D), F32), V((8, D), F32)),
        in_specs=[vspec, pl.BlockSpec(memory_space=pltpu.SMEM), vspec, hspec, hspec, hspec, hspec],
        out_specs=(vspec, vspec, vspec),
        scratch_shapes=scratch,
        compiler_params=pltpu.CompilerParams(
            collective_id=0, has_side_effects=True, vmem_limit_bytes=60 * 1024 * 1024
        ),
        name="layer",
    )(
        item_ids.reshape(1, T), lengths, admitted.reshape(1, R), item_table, input_weight, output_weight, out_grad
    )
    return pl.pallas_call(
        write_out,
        out_shape=(
            jax.ShapeDtypeStruct((T, D), BF16),
            jax.ShapeDtypeStruct((T, D), F32),
            jax.ShapeDtypeStruct((8, D), F32),
        ),
        in_specs=[vspec] * 3,
        out_specs=(hspec,) * 3,
        scratch_shapes=[pltpu.SemaphoreType.DMA((3,))],
        compiler_params=pltpu.CompilerParams(vmem_limit_bytes=16 * 1024 * 1024),
        name="write_out",
    )(*results)


def solution(mesh):
    return jax.shard_map(
        functools.partial(on_device, mesh.shape["dp"]),
        mesh=mesh,
        in_specs=(
            P(("dp", "table")),
            P(("dp", "table"), None),
            P("table", None),
            P("table"),
            P(),
            P(),
            P(("dp", "table"), None),
        ),
        out_specs=(P(("dp", "table"), None), P(("dp", "table"), None), P("table", None)),
        check_vma=False,
    )
```

```python
import functools
import math

import jax
import jax.numpy as jnp
from jax import lax
from jax.experimental import pallas as pl
from jax.experimental.pallas import tpu as pltpu
from jax.sharding import PartitionSpec as P

HEADS = 4
MOST = 128
CAP = 8
NX = 4
EPS = 1e-05
F32 = jnp.float32
BF16 = jnp.bfloat16
MESH = pl.DeviceIdType.MESH


def sigmoid(v):
    return 0.5 * jnp.tanh(0.5 * v) + 0.5


def mm(a, b, dims):
    return lax.dot_general(a, b, (dims, ((), ())), preferred_element_type=F32)


rem = lax.rem


def iota(shape, dim):
    return lax.broadcasted_iota(jnp.int32, shape, dim)


def wait_bytes(ref, sem):
    pltpu.make_async_copy(ref, ref, sem).wait()


def groups(ny):
    return [(1, 7), (4, 3), (5, 2), (6, 0)] if ny == 8 else [((k + 1) % ny,) for k in range(ny)]


def z_split(nz):
    near = 4 if nz % 4 == 0 else 1
    return near, nz // near


def kernel(
    nz, ns,
    ids_hbm, len_hbm, adm_hbm, table_hbm, win_hbm, wout_hbm, og_hbm,
    lo_v, eg_v, wg_v,
    ids_ref, len_ref, adm_ref, table_v, win_v, wout_v, og_v,
    req_s, req_r, flg_s, flg_r, rows_s, rows_r,
    perm, fet_v, nrm_f, nrm_b, proj, act, vism, sco, wts,
    att, hnorm, mix, gmix, gatt, gproj,
    wt_f, w1_s, w1_r, xa1_s, xa1_r, xa2_s, xa2_r, yb_s, yb_r, ya1_s, ya1_r, ya2_s, ya2_r, xb_s, xb_r,
    zr1, zr2, zg1, zg2,
    acc, ld_sem, ss, rs, rs_req, rs_rows, rs1,
):
    ny = ns // (2 * NX)
    row = 2 * NX
    T, D = og_v.shape
    W = wout_v.shape[0]
    R = table_v.shape[0]
    H = D // 2
    hd = W // HEADS
    z = lax.axis_index("dp")
    me = lax.axis_index("table")
    core = rem(me, 2)
    x = rem(me // 2, NX)
    y = me // row
    near, far = z_split(nz)
    zl = z % near
    zg_me = z // near

    def copy(src, dst, i, to, sem=None):
        c = pltpu.make_async_remote_copy(
            src, dst, ss.at[i], rs.at[i] if sem is None else sem, device_id=to, device_id_type=MESH
        )
        c.start()

    bar = pltpu.get_barrier_semaphore()

    def sig_t(k, c):
        pl.semaphore_signal(bar, 1, device_id={"table": rem(me + k, ns)}, device_id_type=MESH)
        return c

    lax.fori_loop(3 * ns // 8, ns, sig_t, 0)
    lax.fori_loop(1, 3 * ns // 8, sig_t, 0)
    near_z = [zg_me * near + (zl + i) % near for i in range(1, near)]
    far_z = [((zg_me + i) % far) * near + zl for i in range(1, far)]
    for to in near_z + far_z:
        pl.semaphore_signal(bar, 1, device_id={"dp": to}, device_id_type=MESH)

    loads = [
        pltpu.make_async_copy(table_hbm, table_v, ld_sem.at[0]),
        pltpu.make_async_copy(wout_hbm, wout_v, ld_sem.at[1]),
        pltpu.make_async_copy(og_hbm, og_v, ld_sem.at[2]),
        pltpu.make_async_copy(win_hbm, win_v, ld_sem.at[3]),
        pltpu.make_async_copy(ids_hbm, ids_ref, ld_sem.at[4]),
        pltpu.make_async_copy(len_hbm, len_ref, ld_sem.at[5]),
        pltpu.make_async_copy(adm_hbm, adm_ref, ld_sem.at[6]),
    ]
    for i in (4, 0, 6, 5):
        loads[i].start()

    loads[4].wait()
    ids_row = ids_ref[...]
    own_row = ids_row >> (R.bit_length() - 1)
    ri = iota((T, T), 0)
    ci = iota((T, T), 1)
    ids_col = jnp.sum(
        jnp.where(ri == ci, jnp.broadcast_to(ids_row.astype(F32), (T, T)), 0.0), axis=1, keepdims=True
    ).astype(jnp.int32)
    own_col = ids_col >> (R.bit_length() - 1)
    loc_col = ids_col & (R - 1)
    before = (own_col == own_row) & (ci < ri)
    rank_col = jnp.sum(jnp.where(before, 1.0, 0.0), axis=1, keepdims=True).astype(jnp.int32)
    owner_hot = jnp.where(iota((ns, T), 0) == own_row, 1.0, 0.0).astype(BF16)
    at_rank = iota((T, 128), 1) == rank_col
    hi = jnp.where(at_rank, (loc_col >> 5).astype(F32), 0.0).astype(BF16)
    lo = jnp.where(at_rank, (loc_col & 31).astype(F32), 0.0).astype(BF16)
    req = mm(owner_hot, hi, ((1,), (0,))) * 32.0 + mm(owner_hot, lo, ((1,), (0,)))
    for s in range(ns):
        req_s[s] = req[s : s + 1, :]
    req_r[me] = req_s[me]

    pl.semaphore_wait(bar, ns - 1 + len(near_z) + len(far_z))

    for gi, dys in enumerate(groups(ny)):
        for dy in dys:

            def send_req(k, c):
                peer = rem(y + ny - dy, ny) * row + rem(me + k, row)
                copy(req_s.at[peer], req_r.at[me], 0, {"table": peer}, rs_req.at[gi])
                return c

            lax.fori_loop(0 if dy else 1, row, send_req, 0)

    for i in (1, 2, 3):
        loads[i].start()

    loads[0].wait()
    loads[6].wait()
    adm = adm_ref[...].astype(F32)
    ones = jnp.ones((R, 128), BF16)
    for gi, dys in enumerate(groups(ny)):
        n = len(dys)
        wait_bytes(req_r.at[pl.ds(0, n * row - (0 in dys))], rs_req.at[gi])
        hot = []
        for dy in dys:
            yy = rem(y + dy, ny)
            r = jnp.broadcast_to(req_r[pl.ds(yy * row, row)], (row, CAP, 128))
            r = jnp.where(iota((row, CAP, 128), 1) == iota((row, CAP, 128), 2), r, 0.0)
            r = jnp.sum(r, axis=2, keepdims=True).reshape(row * CAP, 1).astype(jnp.int32)
            hot.append(jnp.where(iota((row * CAP, R), 1) == r, adm, 0.0).astype(BF16))
        hot = jnp.concatenate(hot, axis=0)
        got = mm(hot, table_v[...], ((1,), (0,)))
        got = jnp.concatenate(
            [got[:, :H].reshape(n * row, CAP, H), got[:, H:].reshape(n * row, CAP, H)], axis=1
        ).astype(BF16)
        for j, dy in enumerate(dys):
            yy = rem(y + dy, ny)
            rows_s[pl.ds(yy * row, row)] = got[j * row : (j + 1) * row]

        for dy in dys:

            def send_rows(k, c):
                peer = rem(y + dy, ny) * row + rem(me + k, row)
                copy(rows_s.at[peer], rows_r.at[me], 1, {"table": peer}, rs_rows.at[gi])
                return c

            lax.fori_loop(0 if dy else 1, row, send_rows, 0)
        flg = mm(hot, ones, ((1,), (0,))).reshape(n * row, CAP, 128)
        flg = jnp.where(iota(flg.shape, 1) == iota(flg.shape, 2), flg, 0.0)
        flg = jnp.sum(flg, axis=1, keepdims=True)
        for j, dy in enumerate(dys):
            yy = rem(y + dy, ny)
            flg_s[pl.ds(yy * row, row)] = flg[j * row : (j + 1) * row]

    def send_flg(k, c):
        peer = rem(me + k, ns)
        copy(flg_s.at[peer], flg_r.at[me], 2, {"table": peer})
        return c

    lax.fori_loop(1, ns, send_flg, 0)
    rows_r[me] = rows_s[me]
    flg_r[me] = flg_s[me]

    slot = own_col * (2 * CAP) + rank_col
    pi = iota((T, ns * 2 * CAP), 1)
    perm[pl.ds(0, T)] = jnp.where(pi == slot, 1.0, 0.0).astype(BF16)
    perm[pl.ds(T, T)] = jnp.where(pi == slot + CAP, 1.0, 0.0).astype(BF16)

    loads[5].wait()
    l0 = len_ref[:, 0:1]
    l1 = l0 + len_ref[:, 1:2]
    l2 = l1 + len_ref[:, 2:3]

    def segment(pos):
        one = jnp.where(pos >= l0, 1, 0)
        two = jnp.where(pos >= l1, 1, 0)
        return one + two + jnp.where(pos >= l2, 1, 0)

    vism[...] = jnp.where((segment(ri) == segment(ci)) & (ci <= ri), 1.0 / MOST, 0.0)

    loads[1].wait()
    loads[2].wait()
    gmix[...] = mm(og_v[...], wout_v[...], ((1,), (1,)))
    loads[3].wait()

    last = len(groups(ny)) - 1
    for gi, dys in enumerate(groups(ny)):
        wait_bytes(rows_r.at[pl.ds(0, len(dys) * row - (0 in dys))], rs_rows.at[gi])
        got = acc[...] if gi else None
        for dy in dys:
            yy = rem(y + ny - dy, ny)
            wide = row * 2 * CAP
            part = mm(
                perm[:, pl.ds(pl.multiple_of(yy * wide, wide), wide)],
                rows_r[pl.ds(yy * row, row)].reshape(wide, H),
                ((1,), (0,)),
            )
            got = part if got is None else got + part
        if gi < last:
            acc[...] = got
    fet = jnp.concatenate([got[:T], got[T:]], axis=1)
    fet_v[...] = fet
    cen = fet - jnp.sum(fet, axis=1, keepdims=True) * (1.0 / D)
    inv = lax.rsqrt(jnp.sum(cen * cen, axis=1, keepdims=True) * (1.0 / D) + EPS)
    nrm = cen * inv
    nrm_f[...] = nrm
    nrm_b[...] = nrm.astype(BF16)

    wide = min(256, 4 * W)
    for n in range(4 * W // wide):
        cols = slice(n * wide, (n + 1) * wide)
        p = mm(nrm_b[...], win_v[:, cols], ((1,), (0,)))
        proj[:, cols] = p
        act[:, cols] = (p * sigmoid(p)).astype(BF16)

    for h in range(HEADS):
        v = act[:, W + h * hd : W + (h + 1) * hd]
        q = act[:, 2 * W + h * hd : 2 * W + (h + 1) * hd]
        k = act[:, 3 * W + h * hd : 3 * W + (h + 1) * hd]
        s = mm(q, k, ((1,), (1,)))
        sco[h] = s
        w = (s * sigmoid(s) * vism[...]).astype(BF16)
        wts[h] = w
        att[:, h * hd : (h + 1) * hd] = mm(w, v, ((1,), (0,)))

    a = att[...]
    a = a - jnp.sum(a, axis=1, keepdims=True) * (1.0 / W)
    hscale = lax.rsqrt(jnp.sum(a * a, axis=1, keepdims=True) * (1.0 / W) + EPS)
    hn = a * hscale
    hnorm[...] = hn
    mix[...] = (hn * act[:, :W].astype(F32)).astype(BF16)

    factor = 1.0 / math.sqrt(T * nz * ns)
    partner = me + 1 - 2 * core
    Q = H // 2
    E = H // 4
    for c in range(2):
        for h in range(2):
            wt = mm(mix[...], og_v[:, h * H + c * Q : h * H + (c + 1) * Q], ((0,), (0,))) * factor
            wt = wt.reshape(ny, NX, 2, 8, Q)
            for xx in range(NX):
                for cc in range(2):
                    wt_f[c, cc, xx, :, h * 8 : (h + 1) * 8, :] = wt[:, xx, cc]
        for i in range(NX):
            xx = rem(x + NX // 2 + i, NX)
            w1_s[c, xx] = wt_f[c, 1 - core, xx].astype(BF16)
            copy(w1_s.at[c, xx], w1_r.at[c, xx], 3, {"table": partner}, rs1.at[c * NX + xx])

    def along_x(xx):
        return {"table": (y * NX + xx) * 2 + core}

    def along_y(src, dst, i):
        def send(k, c):
            yy = rem(y + k, ny)
            copy(src.at[yy], dst.at[y], i, {"table": (yy * NX + x) * 2 + core})
            return c

        lax.fori_loop(1, ny, send, 0)

    for c in range(2):
        for i in range(NX):
            xx = rem(x + NX // 2 + i, NX)
            wait_bytes(w1_r.at[c, xx], rs1.at[c * NX + xx])
            total = wt_f[c, core, xx] + w1_r[c, xx].astype(F32)
            mine = i == NX - NX // 2
            if c == 0:
                xa1_s[xx] = total.astype(BF16)
                if not mine:
                    copy(xa1_s.at[xx], xa1_r.at[x], 4, along_x(xx))
            else:
                xa2_s[xx] = total[..., :E].astype(BF16)
                if not mine:
                    copy(xa2_s.at[xx], xa2_r.at[x], 5, along_x(xx))
                yb_s[:, xx] = total[..., E:].astype(BF16)
    xa1_r[x] = xa1_s[x]
    xa2_r[x] = xa2_s[x]
    along_y(yb_s, yb_r, 6)
    yb_r[y] = yb_s[y]

    lo_v[...] = (fet_v[...] + mm(mix[...], wout_v[...], ((1,), (0,)))).astype(BF16)

    g = gmix[...] * act[:, :W].astype(F32)
    hn = hnorm[...]
    g = g - jnp.sum(g, axis=1, keepdims=True) * (1.0 / W) - hn * (jnp.sum(g * hn, axis=1, keepdims=True) * (1.0 / W))
    gatt[...] = (hscale * g).astype(BF16)

    def through_silu(grad, at):
        p = proj[:, at : at + grad.shape[1]]
        s = sigmoid(p)
        gproj[:, at : at + grad.shape[1]] = (grad * (s * (1.0 + p * (1.0 - s)))).astype(BF16)

    through_silu(gmix[...] * hn, 0)
    for h in range(HEADS):
        v = act[:, W + h * hd : W + (h + 1) * hd]
        q = act[:, 2 * W + h * hd : 2 * W + (h + 1) * hd]
        k = act[:, 3 * W + h * hd : 3 * W + (h + 1) * hd]
        ga = gatt[:, h * hd : (h + 1) * hd]
        gw = mm(ga, v, ((1,), (1,)))
        gv = mm(wts[h], ga, ((0,), (0,)))
        sv = sco[h]
        s = sigmoid(sv)
        gs = (gw * (s * (1.0 + sv * (1.0 - s))) * vism[...]).astype(BF16)
        gq = mm(gs, k, ((1,), (0,)))
        gk = mm(gs, q, ((0,), (0,)))
        through_silu(gv, W + h * hd)
        through_silu(gq, 2 * W + h * hd)
        through_silu(gk, 3 * W + h * hd)

    def add_up(ref, n):
        total = ref[0].astype(F32)
        for i in range(1, n):
            total = total + ref[i].astype(F32)
        return total.astype(BF16)

    wait_bytes(xa1_r.at[pl.ds(0, NX - 1)], rs.at[4])
    ya1_s[...] = add_up(xa1_r, NX)
    along_y(ya1_s, ya1_r, 7)
    ya1_r[y] = ya1_s[y]
    wait_bytes(xa2_r.at[pl.ds(0, NX - 1)], rs.at[5])
    ya2_s[...] = add_up(xa2_r, NX)
    along_y(ya2_s, ya2_r, 8)
    ya2_r[y] = ya2_s[y]
    wait_bytes(yb_r.at[pl.ds(0, ny - 1)], rs.at[6])
    xb_s[...] = add_up(yb_r, ny)
    for i in range(1, NX):
        xx = rem(x + i, NX)
        copy(xb_s.at[xx], xb_r.at[x], 9, along_x(xx))
    xb_r[x] = xb_s[x]

    gn = mm(gproj[...], win_v[...], ((1,), (1,)))
    nrm = nrm_f[...]
    m1 = jnp.sum(gn, axis=1, keepdims=True) * (1.0 / D)
    m2 = jnp.sum(gn * nrm, axis=1, keepdims=True) * (1.0 / D)
    wait_bytes(flg_r.at[pl.ds(0, ns - 1)], rs.at[2])
    flags = jnp.concatenate([flg_r[s] for s in range(ns)], axis=0).astype(BF16)
    own_hot = jnp.where(iota((T, ns), 1) == own_col, 1.0, 0.0).astype(BF16)
    flag = mm(own_hot, flags, ((1,), (0,)))
    flag = jnp.sum(jnp.where(at_rank, flag, 0.0), axis=1, keepdims=True)
    eg_v[...] = flag * (inv * (gn - m1 - nrm * m2) + og_v[...].astype(F32))

    def to_near(ref, i):
        for to in near_z:
            copy(ref.at[zl], ref.at[zl], i, {"dp": to})

    def to_far(ref, src, i):
        if near > 1:
            wait_bytes(src.at[pl.ds(0, near - 1)], rs.at[i])
        ref[zg_me] = add_up(src, near)
        for to in far_z:
            copy(ref.at[zg_me], ref.at[zg_me], i + 2, {"dp": to})

    wait_bytes(ya1_r.at[pl.ds(0, ny - 1)], rs.at[7])
    zr1[zl] = add_up(ya1_r, ny)
    to_near(zr1, 10)
    wait_bytes(ya2_r.at[pl.ds(0, ny - 1)], rs.at[8])
    zr2[zl, :, pl.ds(0, E)] = add_up(ya2_r, ny)
    wait_bytes(xb_r.at[pl.ds(0, NX - 1)], rs.at[9])
    zr2[zl, :, pl.ds(E, E)] = add_up(xb_r, NX)
    to_near(zr2, 11)
    to_far(zg1, zr1, 10)
    to_far(zg2, zr2, 11)
    for c, ref in enumerate((zg1, zg2)):
        if far > 1:
            wait_bytes(ref.at[pl.ds(0, far - 1)], rs.at[12 + c])
        total = ref[0].astype(F32)
        for i in range(1, far):
            total = total + ref[i].astype(F32)
        wg_v[:, c * Q : (c + 1) * Q] = total[:8]
        wg_v[:, H + c * Q : H + (c + 1) * Q] = total[8:]

    wait_bytes(req_s.at[pl.ds(0, ns - 1)], ss.at[0])
    wait_bytes(rows_s.at[pl.ds(0, ns - 1)], ss.at[1])
    wait_bytes(flg_s.at[pl.ds(0, ns - 1)], ss.at[2])
    wait_bytes(w1_s, ss.at[3])
    for i, (ref, n) in enumerate(
        ((xa1_s, NX), (xa2_s, NX), (yb_s, ny), (ya1_s, ny), (ya2_s, ny), (xb_s, NX), (zr1, near), (zr2, near), (zg1, far), (zg2, far))
    ):
        if n > 1:
            wait_bytes(ref.at[pl.ds(0, n - 1)], ss.at[4 + i])


def write_out(lo, eg, wg, lo_out, eg_out, wg_out, sems):
    n = lo.shape[0] // 4
    copies = [(eg.at[pl.ds(i * n, n)], eg_out.at[pl.ds(i * n, n)]) for i in range(4)]
    copies += [(lo.at[pl.ds(i * n * 2, n * 2)], lo_out.at[pl.ds(i * n * 2, n * 2)]) for i in range(2)]
    copies = [pltpu.make_async_copy(a, b, sems.at[i]) for i, (a, b) in enumerate(copies + [(wg, wg_out)])]
    for c in copies:
        c.start()
    for c in copies:
        c.wait()


def on_device(nz, item_ids, lengths, item_table, admitted, input_weight, output_weight, out_grad):
    ns = lax.axis_size("table")
    ny = ns // (2 * NX)
    T = item_ids.shape[0]
    R, D = item_table.shape
    W = output_weight.shape[0]
    H = D // 2
    Q = H // 2
    E = H // 4
    near, far = z_split(nz)
    V = pltpu.VMEM
    vspec = pl.BlockSpec(memory_space=pltpu.VMEM)
    hspec = pl.BlockSpec(memory_space=pltpu.HBM)
    scratch = [
        V((1, T), jnp.int32), V((1, 4), jnp.int32), V((1, R), jnp.int32),
        V((R, D), BF16), V((D, 4 * W), BF16), V((W, D), BF16), V((T, D), BF16),
        V((ns, 1, 128), F32), V((ns, 1, 128), F32), V((ns, 1, 128), F32), V((ns, 1, 128), F32),
        V((ns, 2 * CAP, H), BF16), V((ns, 2 * CAP, H), BF16),
        V((2 * T, ns * 2 * CAP), BF16), V((T, D), F32), V((T, D), F32), V((T, D), BF16),
        V((T, 4 * W), F32), V((T, 4 * W), BF16), V((T, T), F32), V((HEADS, T, T), F32), V((HEADS, T, T), BF16),
        V((T, W), F32), V((T, W), F32), V((T, W), BF16), V((T, W), F32), V((T, W), BF16), V((T, 4 * W), BF16),
        V((2, 2, NX, ny, 16, Q), F32), V((2, NX, ny, 16, Q), BF16), V((2, NX, ny, 16, Q), BF16),
        V((NX, ny, 16, Q), BF16), V((NX, ny, 16, Q), BF16), V((NX, ny, 16, E), BF16), V((NX, ny, 16, E), BF16),
        V((ny, NX, 16, E), BF16), V((ny, NX, 16, E), BF16),
        V((ny, 16, Q), BF16), V((ny, 16, Q), BF16), V((ny, 16, E), BF16), V((ny, 16, E), BF16),
        V((NX, 16, E), BF16), V((NX, 16, E), BF16),
        V((near, 16, Q), BF16), V((near, 16, Q), BF16), V((far, 16, Q), BF16), V((far, 16, Q), BF16),
        V((2 * T, H), F32),
        pltpu.SemaphoreType.DMA((7,)),
        pltpu.SemaphoreType.DMA((14,)), pltpu.SemaphoreType.DMA((14,)),
        pltpu.SemaphoreType.DMA((len(groups(ny)),)), pltpu.SemaphoreType.DMA((len(groups(ny)),)), pltpu.SemaphoreType.DMA((2 * NX,)),
    ]
    results = pl.pallas_call(
        functools.partial(kernel, nz, ns),
        out_shape=(V((T, D), BF16), V((T, D), F32), V((8, D), F32)),
        in_specs=[hspec] * 7,
        out_specs=(vspec, vspec, vspec),
        scratch_shapes=scratch,
        compiler_params=pltpu.CompilerParams(
            collective_id=0, has_side_effects=True, vmem_limit_bytes=60 * 1024 * 1024
        ),
        name="layer",
    )(
        item_ids.reshape(1, T), lengths, admitted.reshape(1, R), item_table, input_weight, output_weight, out_grad
    )
    return pl.pallas_call(
        write_out,
        out_shape=(
            jax.ShapeDtypeStruct((T, D), BF16),
            jax.ShapeDtypeStruct((T, D), F32),
            jax.ShapeDtypeStruct((8, D), F32),
        ),
        in_specs=[vspec] * 3,
        out_specs=(hspec,) * 3,
        scratch_shapes=[pltpu.SemaphoreType.DMA((7,))],
        compiler_params=pltpu.CompilerParams(vmem_limit_bytes=16 * 1024 * 1024),
        name="write_out",
    )(*results)


def solution(mesh):
    return jax.shard_map(
        functools.partial(on_device, mesh.shape["dp"]),
        mesh=mesh,
        in_specs=(
            P(("dp", "table")),
            P(("dp", "table"), None),
            P("table", None),
            P("table"),
            P(),
            P(),
            P(("dp", "table"), None),
        ),
        out_specs=(P(("dp", "table"), None), P(("dp", "table"), None), P("table", None)),
        check_vma=False,
    )
```

```python
import functools
import math

import jax
import jax.numpy as jnp
from jax import lax
from jax.experimental import pallas as pl
from jax.experimental.pallas import tpu as pltpu
from jax.sharding import PartitionSpec as P

HEADS = 4
MOST = 128
CAP = 8
NX = 4
EPS = 1e-05
F32 = jnp.float32
BF16 = jnp.bfloat16
MESH = pl.DeviceIdType.MESH


def sigmoid(v):
    return 0.5 * jnp.tanh(0.5 * v) + 0.5


def mm(a, b, dims):
    return lax.dot_general(a, b, (dims, ((), ())), preferred_element_type=F32)


rem = lax.rem


def iota(shape, dim):
    return lax.broadcasted_iota(jnp.int32, shape, dim)


def wait_bytes(ref, sem):
    pltpu.make_async_copy(ref, ref, sem).wait()


def groups(ny):
    return [(1, 7), (4, 3), (5, 2), (6, 0)] if ny == 8 else [((k + 1) % ny,) for k in range(ny)]


def z_split(nz):
    near = 4 if nz % 4 == 0 else 1
    return near, nz // near


def kernel(
    nz, ns,
    ids_hbm, len_hbm, adm_hbm, table_hbm, win_hbm, wout_hbm, og_hbm,
    lo_v, eg_v, wg_v,
    ids_ref, len_ref, adm_ref, table_v, win_v, wout_v, og_v,
    req_s, req_r, flg_s, flg_r, rows_s, rows_r,
    perm, fet_v, nrm_f, nrm_b, proj, act, vism, sco, wts,
    att, hnorm, mix, gmix, gatt, gproj,
    wt_f, w1_s, w1_r, xa1_s, xa1_r, xa2_s, xa2_r, yb_s, yb_r, ya1_s, ya1_r, ya2_s, ya2_r, xb_s, xb_r,
    zr1, zr2, zg1, zg2,
    acc, ld_sem, ss, rs, rs_req, rs_rows, rs1,
):
    ny = ns // (2 * NX)
    row = 2 * NX
    T, D = og_v.shape
    W = wout_v.shape[0]
    R = table_v.shape[0]
    H = D // 2
    hd = W // HEADS
    z = lax.axis_index("dp")
    me = lax.axis_index("table")
    core = rem(me, 2)
    x = rem(me // 2, NX)
    y = me // row
    near, far = z_split(nz)
    zl = z % near
    zg_me = z // near

    def copy(src, dst, i, to, sem=None):
        c = pltpu.make_async_remote_copy(
            src, dst, ss.at[i], rs.at[i] if sem is None else sem, device_id=to, device_id_type=MESH
        )
        c.start()

    bar = pltpu.get_barrier_semaphore()

    def sig_t(k, c):
        pl.semaphore_signal(bar, 1, device_id={"table": rem(me + k, ns)}, device_id_type=MESH)
        return c

    lax.fori_loop(3 * ns // 8, ns, sig_t, 0)
    lax.fori_loop(1, 3 * ns // 8, sig_t, 0)
    near_z = [zg_me * near + (zl + i) % near for i in range(1, near)]
    far_z = [((zg_me + i) % far) * near + zl for i in range(1, far)]
    for to in near_z + far_z:
        pl.semaphore_signal(bar, 1, device_id={"dp": to}, device_id_type=MESH)

    loads = [
        pltpu.make_async_copy(table_hbm, table_v, ld_sem.at[0]),
        pltpu.make_async_copy(wout_hbm, wout_v, ld_sem.at[1]),
        pltpu.make_async_copy(og_hbm, og_v, ld_sem.at[2]),
        pltpu.make_async_copy(win_hbm, win_v, ld_sem.at[3]),
        pltpu.make_async_copy(ids_hbm, ids_ref, ld_sem.at[4]),
        pltpu.make_async_copy(len_hbm, len_ref, ld_sem.at[5]),
        pltpu.make_async_copy(adm_hbm, adm_ref, ld_sem.at[6]),
    ]
    for i in (4, 0, 6, 5):
        loads[i].start()

    loads[4].wait()
    ids_row = ids_ref[...]
    own_row = ids_row >> (R.bit_length() - 1)
    ri = iota((T, T), 0)
    ci = iota((T, T), 1)
    ids_col = jnp.sum(
        jnp.where(ri == ci, jnp.broadcast_to(ids_row.astype(F32), (T, T)), 0.0), axis=1, keepdims=True
    ).astype(jnp.int32)
    own_col = ids_col >> (R.bit_length() - 1)
    loc_col = ids_col & (R - 1)
    before = (own_col == own_row) & (ci < ri)
    rank_col = jnp.sum(jnp.where(before, 1.0, 0.0), axis=1, keepdims=True).astype(jnp.int32)
    owner_hot = jnp.where(iota((ns, T), 0) == own_row, 1.0, 0.0).astype(BF16)
    at_rank = iota((T, 128), 1) == rank_col
    hi = jnp.where(at_rank, (loc_col >> 5).astype(F32), 0.0).astype(BF16)
    lo = jnp.where(at_rank, (loc_col & 31).astype(F32), 0.0).astype(BF16)
    req = mm(owner_hot, hi, ((1,), (0,))) * 32.0 + mm(owner_hot, lo, ((1,), (0,)))
    for s in range(ns):
        req_s[s] = req[s : s + 1, :]
    req_r[me] = req_s[me]

    pl.semaphore_wait(bar, ns - 1 + len(near_z) + len(far_z))

    for gi, dys in enumerate(groups(ny)):
        for dy in dys:

            def send_req(k, c):
                peer = rem(y + ny - dy, ny) * row + rem(me + k, row)
                copy(req_s.at[peer], req_r.at[me], 0, {"table": peer}, rs_req.at[gi])
                return c

            lax.fori_loop(0 if dy else 1, row, send_req, 0)

    for i in (1, 2, 3):
        loads[i].start()

    loads[0].wait()
    loads[6].wait()
    adm = adm_ref[...].astype(F32)
    ones = jnp.ones((R, 128), BF16)
    for gi, dys in enumerate(groups(ny)):
        n = len(dys)
        wait_bytes(req_r.at[pl.ds(0, n * row - (0 in dys))], rs_req.at[gi])
        hot = []
        for dy in dys:
            yy = rem(y + dy, ny)
            r = jnp.broadcast_to(req_r[pl.ds(yy * row, row)], (row, CAP, 128))
            r = jnp.where(iota((row, CAP, 128), 1) == iota((row, CAP, 128), 2), r, 0.0)
            r = jnp.sum(r, axis=2, keepdims=True).reshape(row * CAP, 1).astype(jnp.int32)
            hot.append(jnp.where(iota((row * CAP, R), 1) == r, adm, 0.0).astype(BF16))
        hot = jnp.concatenate(hot, axis=0)
        got = mm(hot, table_v[...], ((1,), (0,)))
        got = jnp.concatenate(
            [got[:, :H].reshape(n * row, CAP, H), got[:, H:].reshape(n * row, CAP, H)], axis=1
        ).astype(BF16)
        for j, dy in enumerate(dys):
            yy = rem(y + dy, ny)
            rows_s[pl.ds(yy * row, row)] = got[j * row : (j + 1) * row]

        for dy in dys:

            def send_rows(k, c):
                peer = rem(y + dy, ny) * row + rem(me + k, row)
                copy(rows_s.at[peer], rows_r.at[me], 1, {"table": peer}, rs_rows.at[gi])
                return c

            lax.fori_loop(0 if dy else 1, row, send_rows, 0)
        flg = mm(hot, ones, ((1,), (0,))).reshape(n * row, CAP, 128)
        flg = jnp.where(iota(flg.shape, 1) == iota(flg.shape, 2), flg, 0.0)
        flg = jnp.sum(flg, axis=1, keepdims=True)
        for j, dy in enumerate(dys):
            yy = rem(y + dy, ny)
            flg_s[pl.ds(yy * row, row)] = flg[j * row : (j + 1) * row]

    def send_flg(k, c):
        peer = rem(me + k, ns)
        copy(flg_s.at[peer], flg_r.at[me], 2, {"table": peer})
        return c

    lax.fori_loop(1, ns, send_flg, 0)
    rows_r[me] = rows_s[me]
    flg_r[me] = flg_s[me]

    slot = own_col * (2 * CAP) + rank_col
    pi = iota((T, ns * 2 * CAP), 1)
    perm[pl.ds(0, T)] = jnp.where(pi == slot, 1.0, 0.0).astype(BF16)
    perm[pl.ds(T, T)] = jnp.where(pi == slot + CAP, 1.0, 0.0).astype(BF16)

    loads[5].wait()
    l0 = len_ref[:, 0:1]
    l1 = l0 + len_ref[:, 1:2]
    l2 = l1 + len_ref[:, 2:3]

    def segment(pos):
        one = jnp.where(pos >= l0, 1, 0)
        two = jnp.where(pos >= l1, 1, 0)
        return one + two + jnp.where(pos >= l2, 1, 0)

    vism[...] = jnp.where((segment(ri) == segment(ci)) & (ci <= ri), 1.0 / MOST, 0.0)

    loads[1].wait()
    loads[2].wait()
    gmix[...] = mm(og_v[...], wout_v[...], ((1,), (1,)))
    loads[3].wait()

    last = len(groups(ny)) - 1
    for gi, dys in enumerate(groups(ny)):
        wait_bytes(rows_r.at[pl.ds(0, len(dys) * row - (0 in dys))], rs_rows.at[gi])
        got = acc[...] if gi else None
        for dy in dys:
            yy = rem(y + ny - dy, ny)
            wide = row * 2 * CAP
            part = mm(
                perm[:, pl.ds(pl.multiple_of(yy * wide, wide), wide)],
                rows_r[pl.ds(yy * row, row)].reshape(wide, H),
                ((1,), (0,)),
            )
            got = part if got is None else got + part
        if gi < last:
            acc[...] = got
    fet = jnp.concatenate([got[:T], got[T:]], axis=1)
    fet_v[...] = fet
    cen = fet - jnp.sum(fet, axis=1, keepdims=True) * (1.0 / D)
    inv = lax.rsqrt(jnp.sum(cen * cen, axis=1, keepdims=True) * (1.0 / D) + EPS)
    nrm = cen * inv
    nrm_f[...] = nrm
    nrm_b[...] = nrm.astype(BF16)

    wide = min(256, W)
    first = W // wide
    for n in list(range(first, 4 * first)) + list(range(first)):
        cols = slice(n * wide, (n + 1) * wide)
        p = mm(nrm_b[...], win_v[:, cols], ((1,), (0,)))
        proj[:, cols] = p
        act[:, cols] = (p * sigmoid(p)).astype(BF16)

    for h in range(HEADS):
        v = act[:, W + h * hd : W + (h + 1) * hd]
        q = act[:, 2 * W + h * hd : 2 * W + (h + 1) * hd]
        k = act[:, 3 * W + h * hd : 3 * W + (h + 1) * hd]
        s = mm(q, k, ((1,), (1,)))
        sco[h] = s
        w = (s * sigmoid(s) * vism[...]).astype(BF16)
        wts[h] = w
        att[:, h * hd : (h + 1) * hd] = mm(w, v, ((1,), (0,)))

    a = att[...]
    a = a - jnp.sum(a, axis=1, keepdims=True) * (1.0 / W)
    hscale = lax.rsqrt(jnp.sum(a * a, axis=1, keepdims=True) * (1.0 / W) + EPS)
    hn = a * hscale
    hnorm[...] = hn
    mix[...] = (hn * act[:, :W].astype(F32)).astype(BF16)

    factor = 1.0 / math.sqrt(T * nz * ns)
    partner = me + 1 - 2 * core
    Q = H // 2
    E = H // 4
    for c in range(2):
        for h in range(2):
            wt = mm(mix[...], og_v[:, h * H + c * Q : h * H + (c + 1) * Q], ((0,), (0,))) * factor
            wt = wt.reshape(ny, NX, 2, 8, Q)
            for xx in range(NX):
                for cc in range(2):
                    wt_f[c, cc, xx, :, h * 8 : (h + 1) * 8, :] = wt[:, xx, cc]
        for i in range(NX):
            xx = rem(x + NX // 2 + i, NX)
            w1_s[c, xx] = wt_f[c, 1 - core, xx].astype(BF16)
            copy(w1_s.at[c, xx], w1_r.at[c, xx], 3, {"table": partner}, rs1.at[c * NX + xx])

    def along_x(xx):
        return {"table": (y * NX + xx) * 2 + core}

    def along_y(src, dst, i):
        def send(k, c):
            yy = rem(y + k, ny)
            copy(src.at[yy], dst.at[y], i, {"table": (yy * NX + x) * 2 + core})
            return c

        lax.fori_loop(1, ny, send, 0)

    for c in range(2):
        for i in range(NX):
            xx = rem(x + NX // 2 + i, NX)
            wait_bytes(w1_r.at[c, xx], rs1.at[c * NX + xx])
            total = wt_f[c, core, xx] + w1_r[c, xx].astype(F32)
            mine = i == NX - NX // 2
            if c == 0:
                xa1_s[xx] = total.astype(BF16)
                if not mine:
                    copy(xa1_s.at[xx], xa1_r.at[x], 4, along_x(xx))
            else:
                xa2_s[xx] = total[..., :E].astype(BF16)
                if not mine:
                    copy(xa2_s.at[xx], xa2_r.at[x], 5, along_x(xx))
                yb_s[:, xx] = total[..., E:].astype(BF16)
    xa1_r[x] = xa1_s[x]
    xa2_r[x] = xa2_s[x]
    along_y(yb_s, yb_r, 6)
    yb_r[y] = yb_s[y]

    lo_v[...] = (fet_v[...] + mm(mix[...], wout_v[...], ((1,), (0,)))).astype(BF16)

    g = gmix[...] * act[:, :W].astype(F32)
    hn = hnorm[...]
    g = g - jnp.sum(g, axis=1, keepdims=True) * (1.0 / W) - hn * (jnp.sum(g * hn, axis=1, keepdims=True) * (1.0 / W))
    gatt[...] = (hscale * g).astype(BF16)

    def through_silu(grad, at):
        p = proj[:, at : at + grad.shape[1]]
        s = sigmoid(p)
        gproj[:, at : at + grad.shape[1]] = (grad * (s * (1.0 + p * (1.0 - s)))).astype(BF16)

    through_silu(gmix[...] * hn, 0)
    for h in range(HEADS):
        v = act[:, W + h * hd : W + (h + 1) * hd]
        q = act[:, 2 * W + h * hd : 2 * W + (h + 1) * hd]
        k = act[:, 3 * W + h * hd : 3 * W + (h + 1) * hd]
        ga = gatt[:, h * hd : (h + 1) * hd]
        gw = mm(ga, v, ((1,), (1,)))
        gv = mm(wts[h], ga, ((0,), (0,)))
        sv = sco[h]
        s = sigmoid(sv)
        gs = (gw * (s * (1.0 + sv * (1.0 - s))) * vism[...]).astype(BF16)
        gq = mm(gs, k, ((1,), (0,)))
        gk = mm(gs, q, ((0,), (0,)))
        through_silu(gv, W + h * hd)
        through_silu(gq, 2 * W + h * hd)
        through_silu(gk, 3 * W + h * hd)

    def add_up(ref, n):
        total = ref[0].astype(F32)
        for i in range(1, n):
            total = total + ref[i].astype(F32)
        return total.astype(BF16)

    wait_bytes(xa1_r.at[pl.ds(0, NX - 1)], rs.at[4])
    ya1_s[...] = add_up(xa1_r, NX)
    along_y(ya1_s, ya1_r, 7)
    ya1_r[y] = ya1_s[y]
    wait_bytes(xa2_r.at[pl.ds(0, NX - 1)], rs.at[5])
    ya2_s[...] = add_up(xa2_r, NX)
    along_y(ya2_s, ya2_r, 8)
    ya2_r[y] = ya2_s[y]
    wait_bytes(yb_r.at[pl.ds(0, ny - 1)], rs.at[6])
    xb_s[...] = add_up(yb_r, ny)
    for i in range(1, NX):
        xx = rem(x + i, NX)
        copy(xb_s.at[xx], xb_r.at[x], 9, along_x(xx))
    xb_r[x] = xb_s[x]

    gn = mm(gproj[...], win_v[...], ((1,), (1,)))
    nrm = nrm_f[...]
    m1 = jnp.sum(gn, axis=1, keepdims=True) * (1.0 / D)
    m2 = jnp.sum(gn * nrm, axis=1, keepdims=True) * (1.0 / D)
    wait_bytes(flg_r.at[pl.ds(0, ns - 1)], rs.at[2])
    flags = jnp.concatenate([flg_r[s] for s in range(ns)], axis=0).astype(BF16)
    own_hot = jnp.where(iota((T, ns), 1) == own_col, 1.0, 0.0).astype(BF16)
    flag = mm(own_hot, flags, ((1,), (0,)))
    flag = jnp.sum(jnp.where(at_rank, flag, 0.0), axis=1, keepdims=True)
    eg_v[...] = flag * (inv * (gn - m1 - nrm * m2) + og_v[...].astype(F32))

    def to_near(ref, i):
        for to in near_z:
            copy(ref.at[zl], ref.at[zl], i, {"dp": to})

    def to_far(ref, src, i):
        if near > 1:
            wait_bytes(src.at[pl.ds(0, near - 1)], rs.at[i])
        ref[zg_me] = add_up(src, near)
        for to in far_z:
            copy(ref.at[zg_me], ref.at[zg_me], i + 2, {"dp": to})

    wait_bytes(ya1_r.at[pl.ds(0, ny - 1)], rs.at[7])
    zr1[zl] = add_up(ya1_r, ny)
    to_near(zr1, 10)
    wait_bytes(ya2_r.at[pl.ds(0, ny - 1)], rs.at[8])
    zr2[zl, :, pl.ds(0, E)] = add_up(ya2_r, ny)
    wait_bytes(xb_r.at[pl.ds(0, NX - 1)], rs.at[9])
    zr2[zl, :, pl.ds(E, E)] = add_up(xb_r, NX)
    to_near(zr2, 11)
    to_far(zg1, zr1, 10)
    to_far(zg2, zr2, 11)
    for c, ref in enumerate((zg1, zg2)):
        if far > 1:
            wait_bytes(ref.at[pl.ds(0, far - 1)], rs.at[12 + c])
        total = ref[0].astype(F32)
        for i in range(1, far):
            total = total + ref[i].astype(F32)
        wg_v[:, c * Q : (c + 1) * Q] = total[:8]
        wg_v[:, H + c * Q : H + (c + 1) * Q] = total[8:]

    wait_bytes(req_s.at[pl.ds(0, ns - 1)], ss.at[0])
    wait_bytes(rows_s.at[pl.ds(0, ns - 1)], ss.at[1])
    wait_bytes(flg_s.at[pl.ds(0, ns - 1)], ss.at[2])
    wait_bytes(w1_s, ss.at[3])
    for i, (ref, n) in enumerate(
        ((xa1_s, NX), (xa2_s, NX), (yb_s, ny), (ya1_s, ny), (ya2_s, ny), (xb_s, NX), (zr1, near), (zr2, near), (zg1, far), (zg2, far))
    ):
        if n > 1:
            wait_bytes(ref.at[pl.ds(0, n - 1)], ss.at[4 + i])


def write_out(lo, eg, wg, lo_out, eg_out, wg_out, sems):
    n = lo.shape[0] // 4
    copies = [(eg.at[pl.ds(i * n, n)], eg_out.at[pl.ds(i * n, n)]) for i in range(4)]
    copies += [(lo.at[pl.ds(i * n * 2, n * 2)], lo_out.at[pl.ds(i * n * 2, n * 2)]) for i in range(2)]
    copies = [pltpu.make_async_copy(a, b, sems.at[i]) for i, (a, b) in enumerate(copies + [(wg, wg_out)])]
    for c in copies:
        c.start()
    for c in copies:
        c.wait()


def on_device(nz, item_ids, lengths, item_table, admitted, input_weight, output_weight, out_grad):
    ns = lax.axis_size("table")
    ny = ns // (2 * NX)
    T = item_ids.shape[0]
    R, D = item_table.shape
    W = output_weight.shape[0]
    H = D // 2
    Q = H // 2
    E = H // 4
    near, far = z_split(nz)
    V = pltpu.VMEM
    vspec = pl.BlockSpec(memory_space=pltpu.VMEM)
    hspec = pl.BlockSpec(memory_space=pltpu.HBM)
    scratch = [
        V((1, T), jnp.int32), V((1, 4), jnp.int32), V((1, R), jnp.int32),
        V((R, D), BF16), V((D, 4 * W), BF16), V((W, D), BF16), V((T, D), BF16),
        V((ns, 1, 128), F32), V((ns, 1, 128), F32), V((ns, 1, 128), F32), V((ns, 1, 128), F32),
        V((ns, 2 * CAP, H), BF16), V((ns, 2 * CAP, H), BF16),
        V((2 * T, ns * 2 * CAP), BF16), V((T, D), F32), V((T, D), F32), V((T, D), BF16),
        V((T, 4 * W), F32), V((T, 4 * W), BF16), V((T, T), F32), V((HEADS, T, T), F32), V((HEADS, T, T), BF16),
        V((T, W), F32), V((T, W), F32), V((T, W), BF16), V((T, W), F32), V((T, W), BF16), V((T, 4 * W), BF16),
        V((2, 2, NX, ny, 16, Q), F32), V((2, NX, ny, 16, Q), BF16), V((2, NX, ny, 16, Q), BF16),
        V((NX, ny, 16, Q), BF16), V((NX, ny, 16, Q), BF16), V((NX, ny, 16, E), BF16), V((NX, ny, 16, E), BF16),
        V((ny, NX, 16, E), BF16), V((ny, NX, 16, E), BF16),
        V((ny, 16, Q), BF16), V((ny, 16, Q), BF16), V((ny, 16, E), BF16), V((ny, 16, E), BF16),
        V((NX, 16, E), BF16), V((NX, 16, E), BF16),
        V((near, 16, Q), BF16), V((near, 16, Q), BF16), V((far, 16, Q), BF16), V((far, 16, Q), BF16),
        V((2 * T, H), F32),
        pltpu.SemaphoreType.DMA((7,)),
        pltpu.SemaphoreType.DMA((14,)), pltpu.SemaphoreType.DMA((14,)),
        pltpu.SemaphoreType.DMA((len(groups(ny)),)), pltpu.SemaphoreType.DMA((len(groups(ny)),)), pltpu.SemaphoreType.DMA((2 * NX,)),
    ]
    results = pl.pallas_call(
        functools.partial(kernel, nz, ns),
        out_shape=(V((T, D), BF16), V((T, D), F32), V((8, D), F32)),
        in_specs=[hspec] * 7,
        out_specs=(vspec, vspec, vspec),
        scratch_shapes=scratch,
        compiler_params=pltpu.CompilerParams(
            collective_id=0, has_side_effects=True, vmem_limit_bytes=60 * 1024 * 1024
        ),
        name="layer",
    )(
        item_ids.reshape(1, T), lengths, admitted.reshape(1, R), item_table, input_weight, output_weight, out_grad
    )
    return pl.pallas_call(
        write_out,
        out_shape=(
            jax.ShapeDtypeStruct((T, D), BF16),
            jax.ShapeDtypeStruct((T, D), F32),
            jax.ShapeDtypeStruct((8, D), F32),
        ),
        in_specs=[vspec] * 3,
        out_specs=(hspec,) * 3,
        scratch_shapes=[pltpu.SemaphoreType.DMA((7,))],
        compiler_params=pltpu.CompilerParams(vmem_limit_bytes=16 * 1024 * 1024),
        name="write_out",
    )(*results)


def solution(mesh):
    return jax.shard_map(
        functools.partial(on_device, mesh.shape["dp"]),
        mesh=mesh,
        in_specs=(
            P(("dp", "table")),
            P(("dp", "table"), None),
            P("table", None),
            P("table"),
            P(),
            P(),
            P(("dp", "table"), None),
        ),
        out_specs=(P(("dp", "table"), None), P(("dp", "table"), None), P("table", None)),
        check_vma=False,
    )
```
